256 devices in a mesh: ctx: 16 (over z, y_lo), grp: 16 (over y_hi, x, core).
Axes of the slice: x: 4, y: 4 (y_hi: 2, y_lo: 2; y = y_hi * 2 + y_lo), z: 8, core: 2. Of those that a mesh axis runs over, the one named last changes fastest.
Arguments:
- tokens: bfloat16 [32768, 3072], P(('ctx', 'grp')), may hold values from -48 to 48
- w_qkv: bfloat16 [3072, 6144], P(None, 'grp')
- w_out: bfloat16 [2048, 3072], P('grp'), may hold values from -0.125 to 0.125
- source_row: int32 [16, 2048], P('ctx'), may hold values from 0 to 2047, each once within a row
- key_tiles: int32 [256, 30], P('ctx'), may hold values from 0 to 255, as said below
- key_count: int32 [256], P('ctx'), may hold values from 6 to 30
Outputs:
- mixed: bfloat16 [32768, 3072], P(('ctx', 'grp'))
The draws below stay inside these ranges and needn't reach their ends.
Inputs may be any that keep to these rules, and one draw needn't show every extreme that they name: Each row of source_row names every loader row of its tile-frame once. Tile q lies in tile-frame q // 16. key_tiles[q, j] for j < key_count[q] are distinct tiles in tile-frames at most 2 away from q's; entries from key_count[q] on equal q.
All inputs are finite; a program needn't handle non-finite values.
Results may differ from the reference program's by a relative error of at most 0.019.
Values may be sent and summed in bfloat16 or wider, within the bound.
No kernel may reach another device: no remote copies, remote signals or barrier semaphores. Data moves between devices by JAX's collectives and lax.ppermute only.
A program may use at most 64 MiB of HBM per device.

```python
import math
import jax
import jax.numpy as jnp
from jax import lax

D = 3072
HD = 128
HEADS = 16
TH = 2
TW = 8
CG_ROWS = 2048
TILE = 128
QT = 256
REACH = 2
NEIGH = 30
TOKENS = 32768
N_CTX = 16


def draw_tokens(key, part):
    base = jnp.clip(jax.random.normal(jax.random.fold_in(key, 11), (TOKENS, D), jnp.float32), -6.0, 6.0)
    return base.astype(jnp.bfloat16)


def draw_w_qkv(key, part):
    raw_weights = jnp.clip(jax.random.normal(jax.random.fold_in(key, 21), (D, HEADS, 3, HD), jnp.float32), -6.0, 6.0) * D ** (-0.5)
    return raw_weights.reshape(D, HEADS * 3 * HD).astype(jnp.bfloat16)


def mask_lists(key):
    base_key = jax.random.fold_in(key, 7)
    frames = QT // (TH * TW)
    per_frame = TH * TW
    positions = jnp.arange(frames, dtype=jnp.int32)
    cut_draw = jax.random.randint(jax.random.fold_in(base_key, 1), (frames,), 0, 3)
    cuts = jnp.where((cut_draw == 0) & (positions > 2 * REACH), 1, 0).astype(jnp.int32)
    clip_id = jnp.cumsum(cuts)
    tile_ids = jnp.arange(QT, dtype=jnp.int32)
    frame_of = tile_ids // per_frame
    width_of = tile_ids % TW
    offsets = jnp.arange(-REACH, REACH + 1, dtype=jnp.int32)
    frame_cand = frame_of[:, None] + offsets[None, :]
    inside = (frame_cand >= 0) & (frame_cand < frames)
    frame_safe = jnp.clip(frame_cand, 0, frames - 1)
    same_clip = clip_id[frame_safe] == clip_id[frame_of][:, None]
    valid_frame = inside & same_clip
    width_start = jnp.clip(width_of - 1, 0, TW - 3)
    rows_cand = jnp.arange(TH, dtype=jnp.int32)
    cols_cand = jnp.arange(3, dtype=jnp.int32)
    listed = frame_safe[:, :, None, None] * per_frame + rows_cand[None, None, :, None] * TW + width_start[:, None, None, None] + cols_cand[None, None, None, :]
    listed = listed.reshape(QT, NEIGH)
    valid = jnp.broadcast_to(valid_frame[:, :, None, None], (QT, 2 * REACH + 1, TH, 3)).reshape(QT, NEIGH)
    valid_int = valid.astype(jnp.int32)
    noise = jax.random.randint(jax.random.fold_in(base_key, 2), (QT, NEIGH), 0, 65536)
    slot_ids = jnp.arange(NEIGH, dtype=jnp.int32)
    order_key = (1 - valid_int) * 2 ** 24 + noise * NEIGH + slot_ids[None, :]
    ordering = jnp.argsort(order_key, axis=1, stable=True)
    sorted_tiles = jnp.take_along_axis(listed, ordering, axis=1)
    counts = jnp.sum(valid_int, axis=1).astype(jnp.int32)
    filled = jnp.where(slot_ids[None, :] < counts[:, None], sorted_tiles, tile_ids[:, None])
    return (filled.astype(jnp.int32), counts)


def draw_key_tiles(key, part):
    return mask_lists(key)[0]


def draw_key_count(key, part):
    return mask_lists(key)[1]


def block_levels(own_key, dims, shards, least, largest):
    gain = 1.0
    for dim, blocks in shards:
        heights = jax.random.uniform(jax.random.fold_in(jax.random.fold_in(own_key, 6), dim), (blocks,), jnp.float32, least / len(shards), largest / len(shards))
        gain = gain * jnp.repeat(jnp.exp(heights), dims[dim] // blocks).reshape((-1,) + (1,) * (len(dims) - 1 - dim))
    return gain


def bell_draw(stream_key, extent, scale, reach, cuts=(), kind=jnp.bfloat16):
    result = scale * jax.random.normal(stream_key, extent, jnp.float32)
    if cuts:
        result = result * block_levels(stream_key, extent, cuts, -0.22, 0.18)
    return jnp.clip(result, -reach, reach).astype(kind)


def setup_inputs(seed: int = 0) -> dict:
    seeds = jax.random.split(jax.random.key(seed), 7)
    return {
        "tokens": draw_tokens(jax.random.fold_in(seeds[6], 71), 0),
        "w_qkv": draw_w_qkv(jax.random.fold_in(seeds[6], 71), 0),
        "w_out": bell_draw(seeds[2], (HEADS * HD, D), (HEADS * HD) ** -0.5, 0.125, ((0, 16),)),
        "source_row": jax.vmap(lambda own: jax.random.permutation(own, CG_ROWS))(jax.random.split(seeds[3], N_CTX)).reshape((N_CTX, CG_ROWS)).astype(jnp.int32),
        "key_tiles": draw_key_tiles(jax.random.fold_in(seeds[6], 71), 0),
        "key_count": draw_key_count(jax.random.fold_in(seeds[6], 71), 0),
    }


def head_attention(qkv_head, key_tiles, key_count):
    queries = qkv_head[:, :HD].reshape(QT, TILE, HD)
    keys_all = qkv_head[:, HD:2 * HD].reshape(QT, TILE, HD)
    values_all = qkv_head[:, 2 * HD:].reshape(QT, TILE, HD)
    slot_number = jnp.arange(NEIGH * TILE, dtype=jnp.int32) // TILE

    def one_tile(bundle):
        query_tile, listed, counted = bundle
        keys_here = keys_all[listed].reshape(NEIGH * TILE, HD)
        values_here = values_all[listed].reshape(NEIGH * TILE, HD)
        scores = jnp.dot(query_tile, keys_here.T, preferred_element_type=jnp.float32) * (1.0 / math.sqrt(HD))
        scores = jnp.where((slot_number < counted)[None, :], scores, -1e+30)
        row_max = lax.optimization_barrier(jnp.max(scores, axis=1, keepdims=True))
        exponent = jnp.exp(scores - row_max)
        totals = lax.optimization_barrier(jnp.sum(exponent, axis=1, keepdims=True))
        weights = exponent.astype(jnp.bfloat16)
        return (jnp.dot(weights, values_here, preferred_element_type=jnp.float32) / totals).astype(jnp.bfloat16)
    attended = lax.map(one_tile, (queries, key_tiles, key_count))
    return attended.reshape(TOKENS, HD)

def reference(tokens, w_qkv, w_out, source_row, key_tiles, key_count):
    grouped = tokens.reshape(N_CTX, CG_ROWS, D)
    packed = jax.vmap(lambda frame_rows, frame_order: frame_rows[frame_order])(grouped, source_row).reshape(TOKENS, D)
    w_heads = w_qkv.reshape(D, HEADS, 3 * HD).transpose(1, 0, 2)
    out_heads = w_out.reshape(HEADS, HD, D)

    def per_head(running, weights_pair):
        w_one, out_one = weights_pair
        qkv = jnp.dot(packed, w_one, preferred_element_type=jnp.float32).astype(jnp.bfloat16)
        attended = head_attention(qkv, key_tiles, key_count)
        partial_sum = jnp.dot(attended, out_one, preferred_element_type=jnp.float32).astype(jnp.bfloat16)
        partial_sum = lax.optimization_barrier(partial_sum)
        return (running + partial_sum.astype(jnp.float32), None)
    running, _ = lax.scan(per_head, jnp.zeros((TOKENS, D), jnp.float32), (w_heads, out_heads))
    return running.astype(jnp.bfloat16)
```

```python
import functools
import math

import jax
import jax.numpy as jnp
from jax import lax
from jax.experimental import pallas as pl
from jax.experimental.pallas import tpu as pltpu
from jax.sharding import Mesh
from jax.sharding import PartitionSpec as P

BF = jnp.bfloat16
F32 = jnp.float32
TILE = 128
LOG2E = 1.4426950408889634
VM = pltpu.VMEM
SM = pltpu.SMEM
CTX = ("z", "yl")
CHIPS = ("yh", "x")
ALL = ("z", "yl", "yh", "x", "core")
WHOLE_VM = pl.BlockSpec(memory_space=VM)
WHOLE_SM = pl.BlockSpec(memory_space=SM)
WHOLE_ANY = pl.BlockSpec(memory_space=pl.ANY)


def round_x(array, by):
    return lax.ppermute(array, "x", [(i, (i + by) % 4) for i in range(4)])


def swap(array, axis):
    return lax.ppermute(array, axis, [(0, 1), (1, 0)])


def cut(array, dim, start, stop):
    return lax.slice_in_dim(array, start, stop, axis=dim)


def gather_chips(array, dim, first, half_own, half_rest):
    size = array.shape[dim]
    rest = cut(array, dim, first, size)
    far = swap(rest, "yh")

    def along_x(block, half):
        one, three = round_x(block, 1), round_x(block, -1)
        low = round_x(cut(one, dim, 0, half), 1)
        high = round_x(cut(three, dim, half, block.shape[dim]), -1)
        return one, three, low, high

    one, three, low, high = along_x(array, half_own)
    f_one, f_three, f_low, f_high = along_x(far, half_rest)
    out = [(0, 0, 0, size, array), (0, 1, 0, size, one), (0, 3, 0, size, three), (0, 2, 0, half_own, low), (0, 2, half_own, size, high)]
    turn = first + half_rest
    out += [(1, 0, first, size, far), (1, 1, first, size, f_one), (1, 3, first, size, f_three)]
    out += [(1, 2, first, turn, f_low), (1, 2, turn, size, f_high)]
    for dx, block in ((0, array), (1, one), (3, three), (2, low)):
        out.append((1, dx, 0, first, swap(cut(block, dim, 0, first), "yh")))
    return out


def permute_kernel(parts, want_ref, *refs):
    ids, data = refs[:parts], refs[parts : 2 * parts]
    q_ref, kv_ref = refs[2 * parts :]
    rows = 512

    def step(i, carry):
        start = pl.multiple_of(i * rows, rows)
        want = want_ref[pl.ds(start, rows), :]
        picked = None
        for id_ref, data_ref in zip(ids, data):
            hot = jnp.where(want == id_ref[...], 1.0, 0.0).astype(BF)
            part = jnp.dot(hot, data_ref[...], preferred_element_type=F32)
            picked = part if picked is None else picked + part
        picked = picked.astype(BF)
        q_ref[pl.ds(start, rows), :] = picked[:, :TILE]
        kv_ref[pl.ds(start, rows), :] = picked[:, TILE:]
        return carry

    lax.fori_loop(0, q_ref.shape[0] // rows, step, 0)


def permute(want, ids, data):
    n, width = want.shape[0], data[0].shape[1]
    return pl.pallas_call(
        functools.partial(permute_kernel, len(ids)),
        out_shape=(jax.ShapeDtypeStruct((n, TILE), BF), jax.ShapeDtypeStruct((n, width - TILE), BF)),
        in_specs=[WHOLE_VM] * (1 + 2 * len(ids)),
        out_specs=(WHOLE_VM,) * 2,
        compiler_params=pltpu.CompilerParams(vmem_limit_bytes=40 << 20),
        cost_estimate=pl.CostEstimate(flops=2 * n * n * width, bytes_accessed=4 << 20, transcendentals=0),
    )(want, *ids, *data)


def attend_kernel(slots, together, index_ref, count_ref, q_ref, *refs):
    frames = refs[:-4]
    out_ref, win_ref, score_ref, sems = refs[-4:]
    copies = []
    start = 0
    for i, frame in enumerate(frames):
        n = frame.shape[0]
        copies.append(pltpu.make_async_copy(frame, win_ref.at[pl.ds(start, n)], sems.at[i]))
        start += n
    for copy in copies:
        copy.start()
    for copy in copies:
        copy.wait()
    scale = LOG2E / math.sqrt(TILE)

    def tile(t, u):
        base = pl.multiple_of(t * TILE, TILE)
        q = q_ref[pl.ds(base, TILE), :]
        count = count_ref[t]
        top = None
        offs = [pl.multiple_of(index_ref[t, j] * TILE, TILE) for j in range(slots)]
        for j in range(0, slots, 2):
            k = jnp.concatenate([win_ref[pl.ds(offs[j], TILE), :TILE], win_ref[pl.ds(offs[j + 1], TILE), :TILE]], axis=0)
            s = lax.dot_general(q, k, (((1,), (1,)), ((), ())), preferred_element_type=F32)
            for h in range(2):
                part = jnp.where(j + h < count, s[:, h * TILE : (h + 1) * TILE], -1e30)
                score_ref[u, j + h] = part
                top = part if top is None else jnp.maximum(top, part)
        row_max = jnp.max(top, axis=1, keepdims=True) * scale
        total = jnp.zeros((TILE, TILE), F32)
        acc = jnp.zeros((TILE, TILE), F32)
        for j in range(0, slots, 2):
            weights = []
            for h in range(2):
                e = jnp.exp2(score_ref[u, j + h] * scale - row_max)
                total = total + e
                weights.append(e.astype(BF))
            v = jnp.concatenate([win_ref[pl.ds(offs[j], TILE), TILE:], win_ref[pl.ds(offs[j + 1], TILE), TILE:]], axis=0)
            acc = acc + jnp.dot(jnp.concatenate(weights, axis=1), v, preferred_element_type=F32)
        out_ref[pl.ds(base, TILE), :] = (acc / jnp.sum(total, axis=1, keepdims=True)).astype(BF)

    def step(i, carry):
        for u in range(together):
            tile(i * together + u, u)
        return carry

    lax.fori_loop(0, q_ref.shape[0] // TILE // together, step, 0)


def attend(index, count, q, frames):
    n, slots, together = q.shape[0], index.shape[1], 2
    rows = sum(f.shape[0] for f in frames)
    return pl.pallas_call(
        functools.partial(attend_kernel, slots, together),
        out_shape=jax.ShapeDtypeStruct((n, TILE), BF),
        in_specs=[WHOLE_SM] * 2 + [WHOLE_VM] + [WHOLE_ANY] * len(frames),
        out_specs=WHOLE_VM,
        scratch_shapes=[
            VM((rows, 2 * TILE), BF),
            VM((together, slots, TILE, TILE), F32),
            pltpu.SemaphoreType.DMA((len(frames),)),
        ],
        compiler_params=pltpu.CompilerParams(vmem_limit_bytes=40 << 20),
        cost_estimate=pl.CostEstimate(
            flops=4 * n * slots * TILE * TILE, bytes_accessed=6 << 20, transcendentals=n * slots * TILE
        ),
    )(index, count, q, *frames)


def project_kernel(layout, order_ref, att_ref, *refs):
    pieces = refs[: sum(len(p) for p in layout)]
    mine_ref, other_ref = refs[-2:]
    own = pl.multiple_of(order_ref[len(layout)] * TILE, TILE)
    away = pl.multiple_of(TILE - own, TILE)
    mine = jnp.concatenate([att_ref[order_ref[b], pl.ds(own, TILE), :] for b in range(len(layout))], axis=1)
    other = jnp.concatenate([att_ref[order_ref[b], pl.ds(away, TILE), :] for b in range(len(layout))], axis=1)
    left = jnp.concatenate([mine, other], axis=0)
    step = 256
    for column in range(0, mine_ref.shape[1], step):
        blocks, k = [], 0
        for spans in layout:
            for start, stop in spans:
                if start <= column and column + step <= stop:
                    blocks.append(pieces[k][:, column - start : column - start + step])
                k += 1
        assert len(blocks) == len(layout)
        done = jnp.dot(left, jnp.concatenate(blocks, axis=0), preferred_element_type=F32)
        mine_ref[:, column : column + step] = done[:TILE]
        other_ref[:, column : column + step] = done[TILE:].astype(BF)


def project(order, attended, layout, pieces):
    width = max(stop for spans in layout for _, stop in spans)
    return pl.pallas_call(
        functools.partial(project_kernel, layout),
        out_shape=(jax.ShapeDtypeStruct((TILE, width), F32), jax.ShapeDtypeStruct((TILE, width), BF)),
        in_specs=[WHOLE_SM] + [WHOLE_VM] * (1 + len(pieces)),
        out_specs=(WHOLE_VM,) * 2,
        compiler_params=pltpu.CompilerParams(vmem_limit_bytes=40 << 20),
        cost_estimate=pl.CostEstimate(flops=4 * TILE * 8 * TILE * width, bytes_accessed=10 << 20, transcendentals=0),
    )(order, attended, *pieces)


def body(tokens, w_qkv, w_out, source_row, key_tiles, key_count):
    rows = tokens.shape[0]
    z, yl = lax.axis_index("z"), lax.axis_index("yl")
    yh, x, core = lax.axis_index("yh"), lax.axis_index("x"), lax.axis_index("core")

    gathered = gather_chips(tokens, 0, 48, 64, 32)
    near, far = gathered[:5], gathered[5:]

    def ids(part, of_core):
        spans = []
        for dy, dx, start, stop, _ in part:
            chip = ((yh + dy) % 2) * 4 + (x + 4 - dx) % 4
            spans.append((chip * 2 + of_core) * rows + jnp.arange(start, stop, dtype=jnp.int32))
        return jnp.concatenate(spans)[None, :]

    w_both = jnp.concatenate([w_qkv, swap(w_qkv, "core")], axis=1)
    width = w_qkv.shape[1]
    all_ids, all_data = [], []
    for part in (near, far):
        block = jnp.concatenate([p[4] for p in part], axis=0)
        made = jnp.dot(block, w_both, preferred_element_type=F32).astype(BF)
        all_ids += [ids(part, core), ids(part, 1 - core)]
        all_data += [made[:, :width], swap(made[:, width:], "core")]
    want = source_row[0][:, None]
    q, kv = permute(want, all_ids, all_data)

    w_late, kv = lax.optimization_barrier((w_out, kv))
    w_blocks = gather_chips(w_late, 1, 1280, 1536, 768)

    group = kv.shape[0]
    half = group // 2
    behind = lax.ppermute(kv, "z", [(i, (i + 1) % 8) for i in range(8)])
    ahead = lax.ppermute(kv, "z", [(i, (i + 7) % 8) for i in range(8)])
    beside = swap(kv, "yl")
    cross_low = swap(jnp.where(yl == 0, ahead, behind)[:half], "yl")
    onward = [(2 * i, 2 * ((i + 1) % 8)) for i in range(8)] + [(2 * i + 1, 2 * ((i + 7) % 8) + 1) for i in range(8)]
    cross_high = lax.ppermute(beside[half:], CTX, onward)
    frames = [behind, beside, kv, ahead, cross_low, cross_high]

    tiles = key_tiles.shape[0]
    relative = key_tiles - ((z * 2 + yl) - 2) * tiles
    frame, inside = relative // tiles, relative % tiles
    place = jnp.where(frame == 0, 0, jnp.where(frame == 2, 2, jnp.where(frame == 4, 3, jnp.where((frame == 1) == (yl == 0), 4, 1))))
    attended = attend(place * tiles + inside, key_count, q, frames)

    pieces = lax.all_to_all(attended.reshape(8, 2 * TILE, TILE), CHIPS, split_axis=0, concat_axis=0, tiled=True)
    blocks = sorted({(dy, dx) for dy, dx, *_ in w_blocks})
    layout = tuple(tuple((s, e) for dy, dx, s, e, _ in w_blocks if (dy, dx) == b) for b in blocks)
    flat = [p for b in blocks for dy, dx, _, _, p in w_blocks if (dy, dx) == b]
    order = jnp.stack([((yh + dy) % 2) * 4 + (x + 4 - dx) % 4 for dy, dx in blocks] + [core]).astype(jnp.int32)
    mine, other = project(order, pieces, layout, flat)
    return (mine + swap(other, "core").astype(F32)).astype(BF)


def solution(mesh):
    fine = Mesh(mesh.devices.reshape(8, 2, 2, 4, 2), ALL)
    in_specs = (
        P(ALL, None),
        P(None, ("yh", "x", "core")),
        P(("yh", "x", "core"), None),
        P(CTX, None),
        P(CTX, None),
        P(CTX),
    )
    return jax.shard_map(body, mesh=fine, in_specs=in_specs, out_specs=P(ALL, None), check_vma=False)
```

```python
import functools
import math

import jax
import jax.numpy as jnp
from jax import lax
from jax.experimental import pallas as pl
from jax.experimental.pallas import tpu as pltpu
from jax.sharding import Mesh
from jax.sharding import PartitionSpec as P

BF = jnp.bfloat16
F32 = jnp.float32
TILE = 128
LOG2E = 1.4426950408889634
VM = pltpu.VMEM
SM = pltpu.SMEM
CTX = ("z", "yl")
CHIPS = ("yh", "x")
ALL = ("z", "yl", "yh", "x", "core")
TURNS = (0, 1, 3, 2)
WHOLE_VM = pl.BlockSpec(memory_space=VM)
WHOLE_SM = pl.BlockSpec(memory_space=SM)
WHOLE_ANY = pl.BlockSpec(memory_space=pl.ANY)


def round_x(array, by):
    return lax.ppermute(array, "x", [(i, (i + by) % 4) for i in range(4)])


def swap(array, axis):
    return lax.ppermute(array, axis, [(0, 1), (1, 0)])


def gather_small(array):
    pair = jnp.concatenate([array, swap(array, "yh")], axis=0)
    turned = [pair if dx == 0 else lax.ppermute(pair, "x", [(i, (i + dx) % 4) for i in range(4)]) for dx in TURNS]
    n = array.shape[0]
    return jnp.concatenate([p[dy * n : (dy + 1) * n] for dy in range(2) for p in turned], axis=0)


def qkv_kernel(heights, own_ref, other_ref, *refs):
    pieces = refs[: len(heights)]
    mine_ref, theirs_ref, rows_ref, sems = refs[len(heights) :]
    copies, start = [], 0
    for i, height in enumerate(heights):
        copies.append(pltpu.make_async_copy(pieces[i], rows_ref.at[pl.ds(start, height)], sems.at[i]))
        start += height
    for copy in copies:
        copy.start()
    for copy in copies:
        copy.wait()
    theirs_ref[...] = jnp.dot(rows_ref[...], other_ref[...], preferred_element_type=F32).astype(BF)
    mine_ref[...] = jnp.dot(rows_ref[...], own_ref[...], preferred_element_type=F32).astype(BF)


def qkv(own, other, pieces):
    heights = tuple(p.shape[0] for p in pieces)
    n, depth, width = sum(heights), own.shape[0], own.shape[1]
    return pl.pallas_call(
        functools.partial(qkv_kernel, heights),
        out_shape=(jax.ShapeDtypeStruct((n, width), BF),) * 2,
        in_specs=[WHOLE_VM] * 2 + [WHOLE_ANY] * len(pieces),
        out_specs=(WHOLE_VM,) * 2,
        scratch_shapes=[VM((n, depth), BF), pltpu.SemaphoreType.DMA((len(pieces),))],
        compiler_params=pltpu.CompilerParams(vmem_limit_bytes=40 << 20),
        cost_estimate=pl.CostEstimate(flops=4 * n * depth * width, bytes_accessed=8 << 20, transcendentals=0),
    )(own, other, *pieces)


def hot_rows(want, frame, block_ref, blocks):
    n = want.shape[0]
    high = jnp.broadcast_to(want[:, 2 * frame : 2 * frame + 1], (n, TILE)).astype(BF)
    low = jnp.broadcast_to(want[:, 2 * frame + 1 : 2 * frame + 2], (n, TILE))
    lane = lax.broadcasted_iota(jnp.int32, (n, TILE), 1).astype(F32)
    inside = jnp.where(low == lane, 1.0, 0.0).astype(BF)
    zero = jnp.zeros((n, TILE), BF)
    return jnp.concatenate(
        [jnp.where(high == block_ref[b].astype(BF), inside, zero) for b in range(blocks)], axis=1
    )


def place_kernel(frames, block_ref, want_ref, *refs):
    data, outs = refs[: 2 * frames], refs[2 * frames :]
    rows = 512
    half = 512

    def step(i, carry):
        start = pl.multiple_of(i * rows, rows)
        want = want_ref[pl.ds(start, rows), :]
        for f in range(frames):
            hot = hot_rows(want, f, block_ref, 8)
            first, second = data[2 * f], data[2 * f + 1]
            done = jnp.dot(hot[:, :half], first[:half, :], preferred_element_type=F32)
            done = done + jnp.dot(hot[:, half:], second[:half, :], preferred_element_type=F32)
            outs[f][pl.ds(start, rows), :] = done.astype(BF)
        return carry

    lax.fori_loop(0, want_ref.shape[0] // rows, step, 0)


def place(blocks, want, data):
    n, frames = want.shape[0], len(data) // 2
    widths = [d.shape[1] for d in data[::2]]
    return pl.pallas_call(
        functools.partial(place_kernel, frames),
        out_shape=tuple(jax.ShapeDtypeStruct((n, w), BF) for w in widths),
        in_specs=[WHOLE_SM] + [WHOLE_VM] * (1 + len(data)),
        out_specs=(WHOLE_VM,) * frames,
        compiler_params=pltpu.CompilerParams(vmem_limit_bytes=48 << 20),
        cost_estimate=pl.CostEstimate(flops=2 * n * n // 2 * sum(widths), bytes_accessed=8 << 20, transcendentals=0),
    )(blocks, want, *data)


def attend_kernel(slots, together, frames, index_ref, count_ref, block_ref, want_ref, *refs):
    data, before = refs[: 2 * frames], refs[2 * frames : 3 * frames]
    out_ref, q_ref, win_ref, score_ref = refs[3 * frames :]
    n = q_ref.shape[0]
    rows = 512
    half = 512

    def fill(i, carry):
        start = pl.multiple_of(i * rows, rows)
        want = want_ref[pl.ds(start, rows), :]
        for f in range(frames):
            hot = hot_rows(want, f, block_ref, 8)
            first, second = data[2 * f], data[2 * f + 1]
            done = jnp.dot(hot[:, :half], first[:half, :], preferred_element_type=F32)
            done = done + jnp.dot(hot[:, half:], second[:half, :], preferred_element_type=F32)
            done = done.astype(BF) + before[f][pl.ds(start, rows), :]
            if f == 0:
                q_ref[pl.ds(start, rows), :] = done[:, :TILE]
                done = done[:, TILE:]
            win_ref[pl.ds(pl.multiple_of(f * n + start, rows), rows), :] = done
        return carry

    lax.fori_loop(0, n // rows, fill, 0)
    scale = LOG2E / math.sqrt(TILE)

    def tile(t, u):
        base = pl.multiple_of(t * TILE, TILE)
        q = q_ref[pl.ds(base, TILE), :]
        count = count_ref[t]
        top = None
        offs = [pl.multiple_of(index_ref[t, j] * TILE, TILE) for j in range(slots)]
        for j in range(0, slots, 2):
            k = jnp.concatenate([win_ref[pl.ds(offs[j], TILE), :TILE], win_ref[pl.ds(offs[j + 1], TILE), :TILE]], axis=0)
            s = lax.dot_general(q, k, (((1,), (1,)), ((), ())), preferred_element_type=F32)
            for h in range(2):
                part = jnp.where(j + h < count, s[:, h * TILE : (h + 1) * TILE], -1e30)
                score_ref[u, j + h] = part
                top = part if top is None else jnp.maximum(top, part)
        row_max = jnp.max(top, axis=1, keepdims=True) * scale
        total = jnp.zeros((TILE, TILE), F32)
        acc = jnp.zeros((TILE, TILE), F32)
        for j in range(0, slots, 2):
            weights = []
            for h in range(2):
                e = jnp.exp2(score_ref[u, j + h] * scale - row_max)
                total = total + e
                weights.append(e.astype(BF))
            v = jnp.concatenate([win_ref[pl.ds(offs[j], TILE), TILE:], win_ref[pl.ds(offs[j + 1], TILE), TILE:]], axis=0)
            acc = acc + jnp.dot(jnp.concatenate(weights, axis=1), v, preferred_element_type=F32)
        out_ref[pl.ds(base, TILE), :] = (acc / jnp.sum(total, axis=1, keepdims=True)).astype(BF)

    def step(i, carry):
        for u in range(together):
            tile(i * together + u, u)
        return carry

    lax.fori_loop(0, n // TILE // together, step, 0)


def attend(index, count, blocks, want, data, before):
    n, slots, together, frames = want.shape[0], index.shape[1], 2, len(before)
    return pl.pallas_call(
        functools.partial(attend_kernel, slots, together, frames),
        out_shape=jax.ShapeDtypeStruct((n, TILE), BF),
        in_specs=[WHOLE_SM] * 3 + [WHOLE_VM] * (1 + len(data) + frames),
        out_specs=WHOLE_VM,
        scratch_shapes=[
            VM((n, TILE), BF),
            VM((frames * n, 2 * TILE), BF),
            VM((together, slots, TILE, TILE), F32),
        ],
        compiler_params=pltpu.CompilerParams(vmem_limit_bytes=48 << 20),
        cost_estimate=pl.CostEstimate(
            flops=4 * n * slots * TILE * TILE + n * n * 1408, bytes_accessed=9 << 20, transcendentals=n * slots * TILE
        ),
    )(index, count, blocks, want, *data, *before)


def project_kernel(order_ref, att_ref, w_ref, mine_ref, other_ref):
    blocks = w_ref.shape[1]
    own = pl.multiple_of(order_ref[blocks] * TILE, TILE)
    away = pl.multiple_of(TILE - own, TILE)
    mine = jnp.concatenate([att_ref[order_ref[b], pl.ds(own, TILE), :] for b in range(blocks)], axis=1)
    other = jnp.concatenate([att_ref[order_ref[b], pl.ds(away, TILE), :] for b in range(blocks)], axis=1)
    left = jnp.concatenate([mine, other], axis=0)
    step = 256
    for column in range(0, mine_ref.shape[1], step):
        right = jnp.concatenate([w_ref[:, b, :, column : column + step].reshape(TILE, step) for b in range(blocks)], axis=0)
        done = jnp.dot(left, right, preferred_element_type=F32)
        mine_ref[:, column : column + step] = done[:TILE]
        other_ref[:, column : column + step] = done[TILE:].astype(BF)


def project(order, attended, w):
    width = w.shape[-1]
    return pl.pallas_call(
        project_kernel,
        out_shape=(jax.ShapeDtypeStruct((TILE, width), F32), jax.ShapeDtypeStruct((TILE, width), BF)),
        in_specs=[WHOLE_SM] + [WHOLE_VM] * 2,
        out_specs=(WHOLE_VM,) * 2,
        compiler_params=pltpu.CompilerParams(vmem_limit_bytes=40 << 20),
        cost_estimate=pl.CostEstimate(flops=4 * TILE * 8 * TILE * width, bytes_accessed=10 << 20, transcendentals=0),
    )(order, attended, w)


def exchange(payload, yl):
    half = payload.shape[0] // 2 // TILE * TILE
    behind = lax.ppermute(payload, "z", [(i, (i + 1) % 8) for i in range(8)])
    ahead = lax.ppermute(payload, "z", [(i, (i + 7) % 8) for i in range(8)])
    beside = swap(payload, "yl")
    cross_low = swap(jnp.where(yl == 0, ahead[:half], behind[:half]), "yl")
    onward = [(2 * i, 2 * ((i + 1) % 8)) for i in range(8)] + [(2 * i + 1, 2 * ((i + 7) % 8) + 1) for i in range(8)]
    cross_high = lax.ppermute(beside[half:], CTX, onward)
    return behind, beside, ahead, cross_low, cross_high


def body(tokens, w_qkv, w_out, source_row, key_tiles, key_count):
    z, yl = lax.axis_index("z"), lax.axis_index("yl")
    yh, x, core = lax.axis_index("yh"), lax.axis_index("x"), lax.axis_index("core")
    chip_of = [((yh + dy) % 2) * 4 + (x + 4 - dx) % 4 for dy in range(2) for dx in TURNS]

    first, half_rest = 48, 32
    far_own = swap(tokens[first:], "yh")
    one, three = round_x(tokens, 1), round_x(tokens, -1)
    w_other = swap(w_qkv, "core")
    slice_rows = w_out.shape[0] // 8
    w_few = gather_small(lax.dynamic_slice_in_dim(w_out, z * slice_rows, slice_rows, 0))
    w_all = lax.all_gather(w_few, "z", axis=0, tiled=True).reshape(8, 8, slice_rows, w_out.shape[1])

    half = tokens.shape[0] // 2
    low, high = round_x(one[:half], 1), round_x(three[half:], -1)
    f_one, f_three = round_x(far_own, 1), round_x(far_own, -1)
    f_low, f_high = round_x(f_one[:half_rest], 1), round_x(f_three[half_rest:], -1)
    near_mine, near_theirs = qkv(w_qkv, w_other, [tokens, one, three, low, high])
    near_other = swap(near_theirs, "core")
    low_top, _ = lax.optimization_barrier((low[:first], near_theirs))
    tops = [swap(b[:first], "yh") for b in (tokens, one, three)] + [swap(low_top, "yh")]

    source = source_row[0]
    tail = jnp.stack([source // TILE, source % TILE]).astype(BF).reshape(-1, 2 * TILE)
    near_kv = jnp.concatenate([near_mine[:, TILE:], near_other[:, TILE:], tail], axis=0)
    near_in = exchange(near_kv, yl)

    far_pieces = [tops[0], far_own, tops[1], f_one, tops[2], f_three, tops[3], f_low, f_high]
    far_pieces, _ = lax.optimization_barrier((far_pieces, near_in[:3]))
    far_mine, far_theirs = qkv(w_qkv, w_other, far_pieces)
    far_other = swap(far_theirs, "core")
    far_kv = jnp.concatenate([far_mine[:, TILE:], far_other[:, TILE:]], axis=0)
    far_kv, _ = lax.optimization_barrier((far_kv, near_in[3:]))
    far_in = exchange(far_kv, yl)

    n = near_mine.shape[0]
    def halves(got):
        behind, beside, ahead, low_part, high_part = got
        return [behind[:n], behind[n : 2 * n], beside[:n], beside[n : 2 * n], ahead[:n], ahead[n : 2 * n], low_part, high_part[:n]]

    tails = [tail] + [g[-tail.shape[0] :] for g in (near_in[0], near_in[1], near_in[2], near_in[4])]
    want = jnp.concatenate([t.reshape(2, -1) for t in tails], axis=0).astype(F32).T
    near_blocks = jnp.stack([2 * c + side for side in (core, 1 - core) for c in chip_of[:4]]).astype(F32)
    far_blocks = jnp.stack([2 * c + side for side in (core, 1 - core) for c in chip_of[4:]]).astype(F32)
    before = place(near_blocks, want, [near_mine, near_other] + halves(near_in))

    tiles = key_tiles.shape[0]
    relative = key_tiles - ((z * 2 + yl) - 2) * tiles
    frame, inside = relative // tiles, relative % tiles
    slot = jnp.where(frame == 0, 1, jnp.where(frame == 2, 0, jnp.where(frame == 4, 3, jnp.where((frame == 1) == (yl == 0), 4, 2))))
    attended = attend(slot * tiles + inside, key_count, far_blocks, want, [far_mine, far_other] + halves(far_in), before)

    pieces = lax.all_to_all(attended.reshape(8, 2 * TILE, TILE), CHIPS, split_axis=0, concat_axis=0, tiled=True)
    order = jnp.stack(chip_of + [core]).astype(jnp.int32)
    mine, other = project(order, pieces, w_all)
    return (mine + swap(other, "core").astype(F32)).astype(BF)


def solution(mesh):
    fine = Mesh(mesh.devices.reshape(8, 2, 2, 4, 2), ALL)
    in_specs = (
        P(ALL, None),
        P(None, ("yh", "x", "core")),
        P(("yh", "x", "core"), None),
        P(CTX, None),
        P(CTX, None),
        P(CTX),
    )
    return jax.shard_map(body, mesh=fine, in_specs=in_specs, out_specs=P(ALL, None), check_vma=False)
```

```python
import functools
import math

import jax
import jax.numpy as jnp
from jax import lax
from jax.experimental import pallas as pl
from jax.experimental.pallas import tpu as pltpu
from jax.sharding import Mesh
from jax.sharding import PartitionSpec as P

BF = jnp.bfloat16
F32 = jnp.float32
TILE = 128
LOG2E = 1.4426950408889634
VM = pltpu.VMEM
SM = pltpu.SMEM
CTX = ("z", "yl")
CHIPS = ("yh", "x")
ALL = ("z", "yl", "yh", "x", "core")
NEAR = ((0, 0), (0, 1), (0, 3), (1, 0))
FAR = ((0, 2), (1, 1), (1, 3), (1, 2))
WHOLE_VM = pl.BlockSpec(memory_space=VM)
WHOLE_SM = pl.BlockSpec(memory_space=SM)
WHOLE_ANY = pl.BlockSpec(memory_space=pl.ANY)


def round_x(array, by):
    return lax.ppermute(array, "x", [(i, (i + by) % 4) for i in range(4)])


def swap(array, axis):
    return lax.ppermute(array, axis, [(0, 1), (1, 0)])


def qkv_kernel(heights, own_ref, other_ref, *refs):
    pieces = refs[: len(heights)]
    mine_ref, theirs_ref, rows_ref, sems = refs[len(heights) :]
    copies, start = [], 0
    for i, height in enumerate(heights):
        copies.append(pltpu.make_async_copy(pieces[i], rows_ref.at[pl.ds(start, height)], sems.at[i]))
        start += height
    for copy in copies:
        copy.start()
    for copy in copies:
        copy.wait()
    theirs_ref[...] = jnp.dot(rows_ref[...], other_ref[...], preferred_element_type=F32).astype(BF)
    mine_ref[...] = jnp.dot(rows_ref[...], own_ref[...], preferred_element_type=F32).astype(BF)


def qkv(own, other, pieces):
    heights = tuple(p.shape[0] for p in pieces)
    n, depth, width = sum(heights), own.shape[0], own.shape[1]
    return pl.pallas_call(
        functools.partial(qkv_kernel, heights),
        out_shape=(jax.ShapeDtypeStruct((n, width), BF),) * 2,
        in_specs=[WHOLE_VM] * 2 + [WHOLE_ANY] * len(pieces),
        out_specs=(WHOLE_VM,) * 2,
        scratch_shapes=[VM((n, depth), BF), pltpu.SemaphoreType.DMA((len(pieces),))],
        compiler_params=pltpu.CompilerParams(vmem_limit_bytes=40 << 20),
        cost_estimate=pl.CostEstimate(flops=4 * n * depth * width, bytes_accessed=8 << 20, transcendentals=0),
    )(own, other, *pieces)


def hot_rows(want, block_ref):
    n = want.shape[0]
    high = jnp.broadcast_to(want[:, 0:1], (n, TILE)).astype(BF)
    low = jnp.broadcast_to(want[:, 1:2], (n, TILE))
    lane = lax.broadcasted_iota(jnp.int32, (n, TILE), 1).astype(F32)
    inside = jnp.where(low == lane, 1.0, 0.0).astype(BF)
    zero = jnp.zeros((n, TILE), BF)
    picks = [jnp.where(high == block_ref[b].astype(BF), inside, zero) for b in range(block_ref.shape[0])]
    return jnp.concatenate(picks, axis=1)


def pick(want, block_ref, first_ref, second_ref):
    hot, half = hot_rows(want, block_ref), first_ref.shape[0]
    done = jnp.dot(hot[:, :half], first_ref[...], preferred_element_type=F32)
    return done + jnp.dot(hot[:, half:], second_ref[...], preferred_element_type=F32)


def place_near_kernel(block_ref, want_ref, first_ref, second_ref, out_ref):
    rows = 512

    def step(i, carry):
        spot = pl.ds(pl.multiple_of(i * rows, rows), rows)
        out_ref[spot, :] = pick(want_ref[spot, :], block_ref, first_ref, second_ref).astype(BF)
        return carry

    lax.fori_loop(0, want_ref.shape[0] // rows, step, 0)


def place_far_kernel(block_ref, want_ref, first_ref, second_ref, near_ref, q_ref, kv_ref):
    rows = 512

    def step(i, carry):
        start = pl.multiple_of(i * rows, rows)
        spot = pl.ds(start, rows)
        done = pick(want_ref[spot, :], block_ref, first_ref, second_ref) + near_ref[spot, :].astype(F32)
        q_ref[spot, :] = done[:, :TILE].astype(BF)
        kv_ref[spot, TILE:] = done[:, 2 * TILE :].astype(BF)
        for t in range(0, rows, TILE):
            keys = done[t : t + TILE, TILE : 2 * TILE]
            kv_ref[pl.ds(pl.multiple_of(start + t, TILE), TILE), :TILE] = keys.T.astype(BF)
        return carry

    lax.fori_loop(0, want_ref.shape[0] // rows, step, 0)


def place(blocks, want, first, second, near=None):
    n, width = want.shape[0], first.shape[1]
    if near is None:
        kernel, out = place_near_kernel, jax.ShapeDtypeStruct((n, width), BF)
    else:
        kernel = place_far_kernel
        out = (jax.ShapeDtypeStruct((n, TILE), BF), jax.ShapeDtypeStruct((n, width - TILE), BF))
    operands = (want, first, second) + (() if near is None else (near,))
    return pl.pallas_call(
        kernel,
        out_shape=out,
        in_specs=[WHOLE_SM] + [WHOLE_VM] * len(operands),
        out_specs=WHOLE_VM if near is None else (WHOLE_VM,) * 2,
        compiler_params=pltpu.CompilerParams(vmem_limit_bytes=40 << 20),
        cost_estimate=pl.CostEstimate(flops=n * n * width, bytes_accessed=4 << 20, transcendentals=0),
    )(blocks, *operands)


def attend_kernel(sizes, together, parts, last, index_ref, count_ref, q_ref, *refs):
    frames = refs[:parts]
    refs = refs[parts:]
    if last:
        old_ref, stat_ref, out_ref = refs[:3]
    else:
        out_ref, stat_ref = refs[:2]
    win_ref, score_ref, sems = refs[-3:]
    copies, start = [], 0
    for i, frame in enumerate(frames):
        copies.append(pltpu.make_async_copy(frame, win_ref.at[pl.ds(start, frame.shape[0])], sems.at[i]))
        start += frame.shape[0]
    for copy in copies:
        copy.start()
    for copy in copies:
        copy.wait()
    scale = LOG2E / math.sqrt(TILE)

    ones = jnp.ones((2 * TILE, TILE), BF)
    none = jnp.zeros((TILE, TILE), BF)

    def look(t, u, slots):
        q = q_ref[pl.ds(pl.multiple_of(t * TILE, TILE), TILE), :]
        top = None
        for j in range(0, slots, 2):
            spots = [pl.multiple_of(index_ref[t, j + h] * TILE, TILE) for h in range(2)]
            k = jnp.concatenate([win_ref[pl.ds(s, TILE), :TILE] for s in spots], axis=1)
            s = jnp.dot(q, k, preferred_element_type=F32)
            score_ref[u, j // 2] = s
            s = jnp.maximum(s[:, :TILE], s[:, TILE:])
            top = s if top is None else jnp.maximum(top, s)
        return jnp.max(top, axis=1, keepdims=True) * scale

    def weigh(t, u, slots, peak):
        base = pl.multiple_of(t * TILE, TILE)
        count = count_ref[t]
        if last:
            old = stat_ref[pl.ds(base, TILE), :]
            before = old[:, 0:1]
            peak = jnp.where(count > 0, jnp.maximum(peak, before), before)
        done = None
        for j in range(0, slots, 2):
            spots = [pl.multiple_of(index_ref[t, j + h] * TILE, TILE) for h in range(2)]
            e = jnp.exp2(score_ref[u, j // 2] * scale - peak).astype(BF)
            e = jnp.concatenate([jnp.where(j + h < count, e[:, h * TILE : (h + 1) * TILE], none) for h in range(2)], axis=1)
            v = jnp.concatenate([win_ref[pl.ds(s, TILE), TILE:] for s in spots], axis=0)
            part = jnp.dot(e, jnp.concatenate([v, ones], axis=1), preferred_element_type=F32)
            done = part if done is None else done + part
        value, total = done[:, :TILE], done[:, TILE:]
        if last:
            shrink = jnp.exp2(before - peak)
            total = total + shrink * old[:, 1:2]
            value = value + shrink * old_ref[pl.ds(base, TILE), :]
            out_ref[pl.ds(base, TILE), :] = (value / total).astype(BF)
        else:
            peak = jnp.where(count > 0, peak, -1e30)
            out_ref[pl.ds(base, TILE), :] = value
            lane = lax.broadcasted_iota(jnp.int32, (TILE, TILE), 1)
            stat_ref[pl.ds(base, TILE), :] = jnp.where(lane == 0, peak, total)

    def step(i, carry):
        tiles = [i * together + u for u in range(together)]
        most = functools.reduce(jnp.maximum, [count_ref[t] for t in tiles])
        for k, slots in enumerate(sizes):
            fits = most <= slots
            if k > 0:
                fits = jnp.logical_and(fits, most > sizes[k - 1])

            @pl.when(fits)
            def _(slots=slots):
                peaks = [look(t, u, slots) for u, t in enumerate(tiles)]
                for u, t in enumerate(tiles):
                    weigh(t, u, slots, peaks[u])

        return carry

    lax.fori_loop(0, q_ref.shape[0] // TILE // together, step, 0)


def attend(index, count, q, frames, sizes, old=None, together=2):
    n, slots = q.shape[0], index.shape[1]
    rows = sum(f.shape[0] for f in frames)
    wide = jax.ShapeDtypeStruct((n, TILE), F32)
    return pl.pallas_call(
        functools.partial(attend_kernel, sizes, together, len(frames), old is not None),
        out_shape=(wide, wide) if old is None else jax.ShapeDtypeStruct((n, TILE), BF),
        in_specs=[WHOLE_SM] * 2 + [WHOLE_VM] + [WHOLE_ANY] * len(frames) + [WHOLE_VM] * (0 if old is None else 2),
        out_specs=(WHOLE_VM,) * 2 if old is None else WHOLE_VM,
        scratch_shapes=[
            VM((rows, 2 * TILE), BF),
            VM((together, sizes[-1] // 2, TILE, 2 * TILE), F32),
            pltpu.SemaphoreType.DMA((len(frames),)),
        ],
        compiler_params=pltpu.CompilerParams(vmem_limit_bytes=40 << 20),
        cost_estimate=pl.CostEstimate(
            flops=12 * 4 * n * slots * TILE * TILE, bytes_accessed=6 << 20, transcendentals=n * slots * TILE
        ),
    )(index, count, q, *frames, *(old or ()))


def project_kernel(att_ref, w_ref, core_ref, mine_ref, other_ref):
    chips = w_ref.shape[1]
    own = pl.multiple_of(core_ref[0] * TILE, TILE)
    away = pl.multiple_of(TILE - own, TILE)
    mine = jnp.concatenate([att_ref[b, pl.ds(own, TILE), :] for b in range(chips)], axis=1)
    other = jnp.concatenate([att_ref[b, pl.ds(away, TILE), :] for b in range(chips)], axis=1)
    left = jnp.concatenate([mine, other], axis=0)
    step = 256
    for column in range(0, mine_ref.shape[1], step):
        right = jnp.concatenate([w_ref[:, b, :, column : column + step].reshape(TILE, step) for b in range(chips)], axis=0)
        done = jnp.dot(left, right, preferred_element_type=F32)
        mine_ref[:, column : column + step] = done[:TILE]
        other_ref[:, column : column + step] = done[TILE:].astype(BF)


def project(attended, w, core):
    width = w.shape[-1]
    return pl.pallas_call(
        project_kernel,
        out_shape=(jax.ShapeDtypeStruct((TILE, width), F32), jax.ShapeDtypeStruct((TILE, width), BF)),
        in_specs=[WHOLE_VM] * 2 + [WHOLE_SM],
        out_specs=(WHOLE_VM,) * 2,
        compiler_params=pltpu.CompilerParams(vmem_limit_bytes=40 << 20),
        cost_estimate=pl.CostEstimate(flops=4 * TILE * 8 * TILE * width, bytes_accessed=10 << 20, transcendentals=0),
    )(attended, w, core.astype(jnp.int32).reshape(1))


def listed(place, chosen, slots):
    before = jnp.arange(place.shape[1])[None, :] < jnp.arange(place.shape[1])[:, None]
    rank = jnp.sum(jnp.where(before[None] & chosen[:, None, :], 1, 0), axis=2)
    count = jnp.sum(chosen.astype(jnp.int32), axis=1)
    lead = jnp.minimum(jnp.arange(slots)[None, :], jnp.maximum(count - 1, 0)[:, None])
    lead = jnp.where(jnp.arange(slots)[None, :] < count[:, None], lead, 0)
    hit = (rank[:, None, :] == lead[:, :, None]) & chosen[:, None, :]
    return jnp.sum(jnp.where(hit, place[:, None, :], 0), axis=2).astype(jnp.int32), count


def body(tokens, w_qkv, w_out, source_row, key_tiles, key_count):
    z, yl = lax.axis_index("z"), lax.axis_index("yl")
    yh, x, core = lax.axis_index("yh"), lax.axis_index("x"), lax.axis_index("core")

    one, three = round_x(tokens, 1), round_x(tokens, -1)
    far_own = swap(tokens, "yh")
    w_other = swap(w_qkv, "core")
    half = tokens.shape[0] // 2
    low, high = round_x(one[:half], 1), round_x(three[half:], -1)
    f_one, f_three = round_x(far_own, 1), round_x(far_own, -1)
    near_mine, near_theirs = qkv(w_qkv, w_other, [tokens, one, three, far_own])
    near_other = swap(near_theirs, "core")
    two = jnp.concatenate([low, high], axis=0)
    far_two = swap(two, "yh")

    share = w_out.shape[0] // 8
    w_share = lax.dynamic_slice_in_dim(w_out, z * share, share, 0)
    w_share, _ = lax.optimization_barrier((w_share, w_other))
    w_share = jnp.broadcast_to(w_share[None], (8,) + w_share.shape)
    w_chips = lax.all_to_all(w_share, CHIPS, split_axis=0, concat_axis=0, tiled=True)
    w_all = lax.all_gather(w_chips.reshape(8 * share, -1), "z", axis=0, tiled=True)
    w_all = w_all.reshape(8, 8, share, w_out.shape[1])

    def blocks(part):
        chips = [((yh + dy) % 2) * 4 + (x + 4 - dx) % 4 for dy, dx in part]
        return jnp.stack([2 * c + side for side in (core, 1 - core) for c in chips]).astype(F32)

    source = source_row[0]
    want = jnp.stack([source // TILE, source % TILE], axis=1).astype(F32)
    near = place(blocks(NEAR), want, near_mine, near_other)
    far_mine, far_theirs = qkv(w_qkv, w_other, [low, high, f_one, f_three, far_two])
    far_other = swap(far_theirs, "core")
    q, kv = place(blocks(FAR), want, far_mine, far_other, near)

    behind = lax.ppermute(kv, "z", [(i, (i + 1) % 8) for i in range(8)])
    ahead = lax.ppermute(kv, "z", [(i, (i + 7) % 8) for i in range(8)])
    beside = swap(kv, "yl")
    mid = kv.shape[0] // 2
    cross_low = swap(jnp.where(yl == 0, ahead[:mid], behind[:mid]), "yl")
    onward = [(2 * i, 2 * ((i + 1) % 8)) for i in range(8)] + [(2 * i + 1, 2 * ((i + 7) % 8) + 1) for i in range(8)]
    cross_high = lax.ppermute(beside[mid:], CTX, onward)

    tiles, slots = key_tiles.shape
    relative = key_tiles - ((z * 2 + yl) - 2) * tiles
    frame, inside = relative // tiles, relative % tiles
    crossing = frame == jnp.where(yl == 0, 1, 3)
    window = jnp.where(frame == 2, 0, jnp.where(frame == 0, 1, jnp.where(frame == 4, 3, 2)))
    valid = jnp.arange(slots)[None, :] < key_count[:, None]
    index, count = listed(window * tiles + inside, valid & ~crossing, slots)
    cross_index, cross_count = listed(inside, valid & crossing, tiles)
    state = attend(index, count, q, [kv, behind, beside, ahead], (24, slots), together=4)
    attended = attend(cross_index, cross_count, q, [cross_low, cross_high], (6, tiles), state, together=4)

    pieces = lax.all_to_all(attended.reshape(8, 2 * TILE, TILE), CHIPS, split_axis=0, concat_axis=0, tiled=True)
    mine, other = project(pieces, w_all, core)
    return (mine + swap(other, "core").astype(F32)).astype(BF)


def solution(mesh):
    fine = Mesh(mesh.devices.reshape(8, 2, 2, 4, 2), ALL)
    in_specs = (
        P(ALL, None),
        P(None, ("yh", "x", "core")),
        P(("yh", "x", "core"), None),
        P(CTX, None),
        P(CTX, None),
        P(CTX),
    )
    return jax.shard_map(body, mesh=fine, in_specs=in_specs, out_specs=P(ALL, None), check_vma=False)
```

```python
import functools
import math

import jax
import jax.numpy as jnp
from jax import lax
from jax.experimental import pallas as pl
from jax.experimental.pallas import tpu as pltpu
from jax.sharding import Mesh
from jax.sharding import PartitionSpec as P

BF = jnp.bfloat16
F32 = jnp.float32
TILE = 128
LOG2E = 1.4426950408889634
VM = pltpu.VMEM
SM = pltpu.SMEM
CTX = ("z", "yl")
CHIPS = ("yh", "x")
ALL = ("z", "yl", "yh", "x", "core")
NEAR = ((0, 0), (0, 1), (0, 3), (1, 0))
FAR = ((0, 2), (1, 1), (1, 3), (1, 2))
WHOLE_VM = pl.BlockSpec(memory_space=VM)
WHOLE_SM = pl.BlockSpec(memory_space=SM)
WHOLE_ANY = pl.BlockSpec(memory_space=pl.ANY)


def round_x(array, by):
    return lax.ppermute(array, "x", [(i, (i + by) % 4) for i in range(4)])


def swap(array, axis):
    return lax.ppermute(array, axis, [(0, 1), (1, 0)])


def qkv_kernel(heights, own_ref, other_ref, *refs):
    pieces = refs[: len(heights)]
    mine_ref, theirs_ref, rows_ref, sems = refs[len(heights) :]
    copies, start = [], 0
    for i, height in enumerate(heights):
        copies.append((pltpu.make_async_copy(pieces[i], rows_ref.at[pl.ds(start, height)], sems.at[i]), start + height))
        start += height
    for copy, _ in copies:
        copy.start()
    part = start // 2
    for low in range(0, start, part):
        for copy, end in copies:
            if low < end <= low + part:
                copy.wait()
        rows = rows_ref[low : low + part, :]
        theirs_ref[low : low + part, TILE:] = jnp.dot(rows, other_ref[:, TILE:], preferred_element_type=F32).astype(BF)
        both = jnp.concatenate([other_ref[:, :TILE], own_ref[:, :TILE]], axis=1)
        both = jnp.dot(rows, both, preferred_element_type=F32).astype(BF)
        theirs_ref[low : low + part, :TILE] = both[:, :TILE]
        mine_ref[low : low + part, :TILE] = both[:, TILE:]
        mine_ref[low : low + part, TILE:] = jnp.dot(rows, own_ref[:, TILE:], preferred_element_type=F32).astype(BF)


def qkv(own, other, pieces):
    heights = tuple(p.shape[0] for p in pieces)
    n, depth, width = sum(heights), own.shape[0], own.shape[1]
    return pl.pallas_call(
        functools.partial(qkv_kernel, heights),
        out_shape=(jax.ShapeDtypeStruct((n, width), BF),) * 2,
        in_specs=[WHOLE_VM] * 2 + [WHOLE_ANY] * len(pieces),
        out_specs=(WHOLE_VM,) * 2,
        scratch_shapes=[VM((n, depth), BF), pltpu.SemaphoreType.DMA((len(pieces),))],
        compiler_params=pltpu.CompilerParams(vmem_limit_bytes=24 << 20),
        cost_estimate=pl.CostEstimate(flops=4 * n * depth * width, bytes_accessed=8 << 20, transcendentals=0),
    )(own, other, *pieces)


def hot_rows(want, block_ref):
    n = want.shape[0]
    want = jnp.broadcast_to(want, (n, TILE))
    high = lax.shift_right_logical(want, 7).astype(F32).astype(BF)
    low = want & (TILE - 1)
    inside = jnp.where(low == lax.broadcasted_iota(jnp.int32, (n, TILE), 1), 1.0, 0.0).astype(BF)
    zero = jnp.zeros((n, TILE), BF)
    picks = [jnp.where(high == block_ref[b].astype(BF), inside, zero) for b in range(block_ref.shape[0])]
    return jnp.concatenate(picks, axis=1)


def pick(want, block_ref, first_ref, second_ref):
    hot, half = hot_rows(want, block_ref), first_ref.shape[0]
    done = jnp.dot(hot[:, :half], first_ref[...], preferred_element_type=F32)
    return done + jnp.dot(hot[:, half:], second_ref[...], preferred_element_type=F32)


def place_near_kernel(block_ref, want_ref, first_ref, second_ref, out_ref):
    rows = 512

    def step(i, carry):
        spot = pl.ds(pl.multiple_of(i * rows, rows), rows)
        out_ref[spot, :] = pick(want_ref[spot, :], block_ref, first_ref, second_ref).astype(BF)
        return carry

    lax.fori_loop(0, want_ref.shape[0] // rows, step, 0)


def place_far_kernel(block_ref, want_ref, first_ref, second_ref, near_ref, q_ref, kv_ref):
    rows = 512

    def step(i, carry):
        start = pl.multiple_of(i * rows, rows)
        spot = pl.ds(start, rows)
        done = pick(want_ref[spot, :], block_ref, first_ref, second_ref) + near_ref[spot, :].astype(F32)
        q_ref[spot, :] = done[:, :TILE].astype(BF)
        kv_ref[spot, TILE:] = done[:, 2 * TILE :].astype(BF)
        for t in range(0, rows, TILE):
            keys = done[t : t + TILE, TILE : 2 * TILE]
            kv_ref[pl.ds(pl.multiple_of(start + t, TILE), TILE), :TILE] = keys.T.astype(BF)
        return carry

    lax.fori_loop(0, want_ref.shape[0] // rows, step, 0)


def place(blocks, want, first, second, near=None):
    n, width = want.shape[0], first.shape[1]
    if near is None:
        kernel, out = place_near_kernel, jax.ShapeDtypeStruct((n, width), BF)
    else:
        kernel = place_far_kernel
        out = (jax.ShapeDtypeStruct((n, TILE), BF), jax.ShapeDtypeStruct((n, width - TILE), BF))
    operands = (want, first, second) + (() if near is None else (near,))
    return pl.pallas_call(
        kernel,
        out_shape=out,
        in_specs=[WHOLE_SM] + [WHOLE_VM] * len(operands),
        out_specs=WHOLE_VM if near is None else (WHOLE_VM,) * 2,
        compiler_params=pltpu.CompilerParams(vmem_limit_bytes=24 << 20),
        cost_estimate=pl.CostEstimate(flops=n * n * width, bytes_accessed=4 << 20, transcendentals=0),
    )(blocks, *operands)


def attend_kernel(sizes, together, parts, last, index_ref, count_ref, q_ref, *refs):
    frames = refs[:parts]
    refs = refs[parts:]
    if last:
        old_ref, stat_ref, out_ref = refs[:3]
    else:
        out_ref, stat_ref = refs[:2]
    win_ref, score_ref, sems = refs[-3:]
    copies, start = [], 0
    for i, frame in enumerate(frames):
        copies.append(pltpu.make_async_copy(frame, win_ref.at[pl.ds(start, frame.shape[0])], sems.at[i]))
        start += frame.shape[0]
    for copy in copies:
        copy.start()
    for copy in copies:
        copy.wait()
    scale = LOG2E / math.sqrt(TILE)

    ones = jnp.ones((2 * TILE, TILE), BF)
    none = jnp.zeros((TILE, TILE), BF)

    def look(t, u, slots):
        q = q_ref[pl.ds(pl.multiple_of(t * TILE, TILE), TILE), :]
        top = None
        for j in range(0, slots, 2):
            spots = [pl.multiple_of(index_ref[t, j + h] * TILE, TILE) for h in range(2)]
            k = jnp.concatenate([win_ref[pl.ds(s, TILE), :TILE] for s in spots], axis=1)
            s = jnp.dot(q, k, preferred_element_type=F32)
            score_ref[u, j // 2] = s
            s = jnp.maximum(s[:, :TILE], s[:, TILE:])
            top = s if top is None else jnp.maximum(top, s)
        return jnp.max(top, axis=1, keepdims=True) * scale

    def weigh(t, u, slots, peak):
        base = pl.multiple_of(t * TILE, TILE)
        count = count_ref[t]
        if last:
            old = stat_ref[pl.ds(base, TILE), :]
            before = old[:, 0:1]
            peak = jnp.where(count > 0, jnp.maximum(peak, before), before)
        done = None
        for j in range(0, slots, 2):
            spots = [pl.multiple_of(index_ref[t, j + h] * TILE, TILE) for h in range(2)]
            e = jnp.exp2(score_ref[u, j // 2] * scale - peak).astype(BF)
            e = jnp.concatenate([jnp.where(j + h < count, e[:, h * TILE : (h + 1) * TILE], none) for h in range(2)], axis=1)
            v = jnp.concatenate([win_ref[pl.ds(s, TILE), TILE:] for s in spots], axis=0)
            part = jnp.dot(e, jnp.concatenate([v, ones], axis=1), preferred_element_type=F32)
            done = part if done is None else done + part
        value, total = done[:, :TILE], done[:, TILE:]
        if last:
            shrink = jnp.exp2(before - peak)
            total = total + shrink * old[:, 1:2]
            value = value + shrink * old_ref[pl.ds(base, TILE), :]
            out_ref[pl.ds(base, TILE), :] = (value / total).astype(BF)
        else:
            peak = jnp.where(count > 0, peak, -1e30)
            out_ref[pl.ds(base, TILE), :] = value
            lane = lax.broadcasted_iota(jnp.int32, (TILE, TILE), 1)
            stat_ref[pl.ds(base, TILE), :] = jnp.where(lane == 0, peak, total)

    def step(i, carry):
        tiles = [i * together + u for u in range(together)]
        most = functools.reduce(jnp.maximum, [count_ref[t] for t in tiles])
        for k, slots in enumerate(sizes):
            fits = most <= slots
            if k > 0:
                fits = jnp.logical_and(fits, most > sizes[k - 1])

            @pl.when(fits)
            def _(slots=slots):
                peaks = [look(t, u, slots) for u, t in enumerate(tiles)]
                for u, t in enumerate(tiles):
                    weigh(t, u, slots, peaks[u])

        return carry

    lax.fori_loop(0, q_ref.shape[0] // TILE // together, step, 0)


def attend(index, count, q, frames, sizes, old=None, together=2):
    n, slots = q.shape[0], index.shape[1]
    rows = sum(f.shape[0] for f in frames)
    wide = jax.ShapeDtypeStruct((n, TILE), F32)
    return pl.pallas_call(
        functools.partial(attend_kernel, sizes, together, len(frames), old is not None),
        out_shape=(wide, wide) if old is None else jax.ShapeDtypeStruct((n, TILE), BF),
        in_specs=[WHOLE_SM] * 2 + [WHOLE_VM] + [WHOLE_ANY] * len(frames) + [WHOLE_VM] * (0 if old is None else 2),
        out_specs=(WHOLE_VM,) * 2 if old is None else WHOLE_VM,
        scratch_shapes=[
            VM((rows, 2 * TILE), BF),
            VM((together, sizes[-1] // 2, TILE, 2 * TILE), F32),
            pltpu.SemaphoreType.DMA((len(frames),)),
        ],
        compiler_params=pltpu.CompilerParams(vmem_limit_bytes=24 << 20),
        cost_estimate=pl.CostEstimate(
            flops=4 * 4 * n * slots * TILE * TILE, bytes_accessed=6 << 20, transcendentals=n * slots * TILE
        ),
    )(index, count, q, *frames, *(old or ()))


def project_kernel(order_ref, att_ref, *refs):
    weights, mine_ref, other_ref = refs[:-2], refs[-2], refs[-1]
    chips = att_ref.shape[0]
    own = pl.multiple_of(order_ref[chips] * TILE, TILE)
    away = pl.multiple_of(TILE - own, TILE)
    mine = jnp.concatenate([att_ref[order_ref[b], pl.ds(own, TILE), :] for b in range(chips)], axis=1)
    other = jnp.concatenate([att_ref[order_ref[b], pl.ds(away, TILE), :] for b in range(chips)], axis=1)
    left = jnp.concatenate([mine, other], axis=0)
    step = 256
    for column in range(0, mine_ref.shape[1], step):
        right = jnp.concatenate([w[:, column : column + step] for w in weights], axis=0)
        done = jnp.dot(left, right, preferred_element_type=F32)
        mine_ref[:, column : column + step] = done[:TILE]
        other_ref[:, column : column + step] = done[TILE:].astype(BF)


def project(order, attended, weights):
    width = weights[0].shape[1]
    return pl.pallas_call(
        project_kernel,
        out_shape=(jax.ShapeDtypeStruct((TILE, width), F32), jax.ShapeDtypeStruct((TILE, width), BF)),
        in_specs=[WHOLE_SM] + [WHOLE_VM] * (1 + len(weights)),
        out_specs=(WHOLE_VM,) * 2,
        compiler_params=pltpu.CompilerParams(vmem_limit_bytes=24 << 20),
        cost_estimate=pl.CostEstimate(flops=4 * TILE * 8 * TILE * width, bytes_accessed=10 << 20, transcendentals=0),
    )(order, attended, *weights)


def listed(place, chosen, slots):
    before = jnp.arange(place.shape[1])[None, :] < jnp.arange(place.shape[1])[:, None]
    rank = jnp.sum(jnp.where(before[None] & chosen[:, None, :], 1, 0), axis=2)
    count = jnp.sum(chosen.astype(jnp.int32), axis=1)
    lead = jnp.minimum(jnp.arange(slots)[None, :], jnp.maximum(count - 1, 0)[:, None])
    lead = jnp.where(jnp.arange(slots)[None, :] < count[:, None], lead, 0)
    hit = (rank[:, None, :] == lead[:, :, None]) & chosen[:, None, :]
    return jnp.sum(jnp.where(hit, place[:, None, :], 0), axis=2).astype(jnp.int32), count


def body(tokens, w_qkv, w_out, source_row, key_tiles, key_count):
    z, yl = lax.axis_index("z"), lax.axis_index("yl")
    yh, x, core = lax.axis_index("yh"), lax.axis_index("x"), lax.axis_index("core")
    after = lax.optimization_barrier

    def chips(part):
        return [((yh + dy) % 2) * 4 + (x + 4 - dx) % 4 for dy, dx in part]

    def blocks(part):
        return jnp.stack([2 * c + side for side in (core, 1 - core) for c in chips(part)]).astype(F32)

    one, three = round_x(tokens, 1), round_x(tokens, -1)
    far_own = swap(tokens, "yh")
    w_other = swap(w_qkv, "core")
    half = tokens.shape[0] // 2
    low, high = round_x(one[:half], 1), round_x(three[half:], -1)
    far_next, _ = after((far_own, (one, three)))
    f_one, f_three = round_x(far_next, 1), round_x(far_next, -1)
    far_two = swap(jnp.concatenate([low, high], axis=0), "yh")
    near_mine, near_theirs = qkv(w_qkv, w_other, [tokens, one, three, far_own])
    near_other = swap(near_theirs, "core")
    want = source_row[0][:, None]
    near = place(blocks(NEAR), want, near_mine, near_other)
    far_two, near = after((far_two, near))
    far_mine, far_theirs = qkv(w_qkv, w_other, [low, high, f_one, f_three, far_two])
    far_other = swap(far_theirs, "core")

    w_start, _ = after((w_out, near))
    w_one, w_three = round_x(w_start, 1), round_x(w_start, -1)
    w_turn, _ = after((w_out, far_two))
    w_two, w_far = round_x(w_turn, 2), lax.ppermute(w_turn, ("yl", "yh"), [(i, 3 - i) for i in range(4)])

    q, kv = place(blocks(FAR), want, far_mine, far_other, near)
    kv, _ = after((kv, (w_one, w_three)))
    behind = lax.ppermute(kv, "z", [(i, (i + 1) % 8) for i in range(8)])
    ahead = lax.ppermute(kv, "z", [(i, (i + 7) % 8) for i in range(8)])
    beside = swap(kv, "yl")

    wf_one, wf_three, wf_two = (round_x(w_far, by) for by in (1, -1, 2))

    mid = kv.shape[0] // 2
    cross_low = swap(jnp.where(yl == 0, ahead[:mid], behind[:mid]), "yl")
    onward = [(2 * i, 2 * ((i + 1) % 8)) for i in range(8)] + [(2 * i + 1, 2 * ((i + 7) % 8) + 1) for i in range(8)]
    cross_high = lax.ppermute(beside[mid:], CTX, onward)

    tiles, slots = key_tiles.shape
    relative = key_tiles - ((z * 2 + yl) - 2) * tiles
    frame, inside = relative // tiles, relative % tiles
    crossing = frame == jnp.where(yl == 0, 1, 3)
    window = jnp.where(frame == 2, 0, jnp.where(frame == 0, 1, jnp.where(frame == 4, 3, 2)))
    valid = jnp.arange(slots)[None, :] < key_count[:, None]
    index, count = listed(window * tiles + inside, valid & ~crossing, slots)
    cross_index, cross_count = listed(inside, valid & crossing, tiles)
    state = attend(index, count, q, [kv, behind, beside, ahead], (24, slots), together=4)
    attended = attend(cross_index, cross_count, q, [cross_low, cross_high], (6, tiles), state, together=4)

    pieces = lax.all_to_all(attended.reshape(8, 2 * TILE, TILE), CHIPS, split_axis=0, concat_axis=0, tiled=True)
    order = jnp.stack(chips(((0, 0), (0, 1), (0, 3), (0, 2), (1, 0), (1, 1), (1, 3), (1, 2))) + [core]).astype(jnp.int32)
    weights = [w_out, w_one, w_three, w_two, w_far, wf_one, wf_three, wf_two]
    mine, other = project(order, pieces, weights)
    return (mine + swap(other, "core").astype(F32)).astype(BF)


def solution(mesh):
    fine = Mesh(mesh.devices.reshape(8, 2, 2, 4, 2), ALL)
    in_specs = (
        P(ALL, None),
        P(None, ("yh", "x", "core")),
        P(("yh", "x", "core"), None),
        P(CTX, None),
        P(CTX, None),
        P(CTX),
    )
    return jax.shard_map(body, mesh=fine, in_specs=in_specs, out_specs=P(ALL, None), check_vma=False)
```

```python
import functools
import math

import jax
import jax.numpy as jnp
from jax import lax
from jax.experimental import pallas as pl
from jax.experimental.pallas import tpu as pltpu
from jax.sharding import Mesh
from jax.sharding import PartitionSpec as P

BF = jnp.bfloat16
F32 = jnp.float32
TILE = 128
LOG2E = 1.4426950408889634
VM = pltpu.VMEM
SM = pltpu.SMEM
CTX = ("z", "yl")
CHIPS = ("yh", "x")
ALL = ("z", "yl", "yh", "x", "core")
NEAR = ((0, 0), (0, 1), (0, 3), (1, 0))
FAR = ((0, 2), (1, 1), (1, 3), (1, 2))
WHOLE_VM = pl.BlockSpec(memory_space=VM)
WHOLE_SM = pl.BlockSpec(memory_space=SM)
WHOLE_ANY = pl.BlockSpec(memory_space=pl.ANY)
WHOLE_HBM = pl.BlockSpec(memory_space=pltpu.HBM)


def in_hbm(arrays):
    return [pltpu.with_memory_space_constraint(a, pltpu.HBM) for a in arrays]


def round_x(array, by):
    return lax.ppermute(array, "x", [(i, (i + by) % 4) for i in range(4)])


def swap(array, axis):
    return lax.ppermute(array, axis, [(0, 1), (1, 0)])


def opposite(array):
    return lax.ppermute(array, ("yl", "yh"), [(i, 3 - i) for i in range(4)])


def qkv_kernel(heights, own_ref, other_ref, *refs):
    pieces = refs[: len(heights)]
    mine_ref, theirs_ref, rows_ref, w_ref, row_sems, w_sems = refs[len(heights) :]
    width, group = own_ref.shape[1], 256
    copies, start = [], 0
    for i, height in enumerate(heights):
        copies.append(pltpu.make_async_copy(pieces[i], rows_ref.at[pl.ds(start, height)], row_sems.at[i]))
        start += height
    spans = [(other_ref, 0, group), (other_ref, group, width), (own_ref, 0, 2 * group - width), (own_ref, 2 * group - width, width)]
    loads, place = [], 0
    for i, (ref, low, high) in enumerate(spans):
        loads.append(pltpu.make_async_copy(ref.at[:, low:high], w_ref.at[:, place : place + high - low], w_sems.at[i]))
        place += high - low
    for copy in loads[:1] + copies + loads[1:]:
        copy.start()
    for copy in copies:
        copy.wait()
    for g, needed in enumerate(((0,), (1, 2), (3,))):
        for i in needed:
            loads[i].wait()
        low, high = g * group, (g + 1) * group
        done = jnp.dot(rows_ref[...], w_ref[:, low:high], preferred_element_type=F32).astype(BF)
        if low < width:
            stop = min(high, width)
            theirs_ref[:, low:stop] = done[:, : stop - low]
        if high > width:
            first = max(low, width)
            mine_ref[:, first - width : high - width] = done[:, first - low :]


def qkv(own, other, pieces):
    heights = tuple(p.shape[0] for p in pieces)
    n, depth, width = sum(heights), own.shape[0], own.shape[1]
    return pl.pallas_call(
        functools.partial(qkv_kernel, heights),
        out_shape=(jax.ShapeDtypeStruct((n, width), BF),) * 2,
        in_specs=[WHOLE_HBM] * 2 + [WHOLE_ANY] * len(pieces),
        out_specs=(WHOLE_VM,) * 2,
        scratch_shapes=[
            VM((n, depth), BF),
            VM((depth, 2 * width), BF),
            pltpu.SemaphoreType.DMA((len(pieces),)),
            pltpu.SemaphoreType.DMA((4,)),
        ],
        compiler_params=pltpu.CompilerParams(vmem_limit_bytes=24 << 20),
        cost_estimate=pl.CostEstimate(flops=4 * n * depth * width, bytes_accessed=8 << 20, transcendentals=0),
    )(*in_hbm((own, other)), *pieces)


def hot_rows(want, block_ref):
    n = want.shape[0]
    want = jnp.broadcast_to(want, (n, TILE))
    high = lax.shift_right_logical(want, 7).astype(F32).astype(BF)
    low = want & (TILE - 1)
    inside = jnp.where(low == lax.broadcasted_iota(jnp.int32, (n, TILE), 1), 1.0, 0.0).astype(BF)
    zero = jnp.zeros((n, TILE), BF)
    picks = [jnp.where(high == block_ref[b].astype(BF), inside, zero) for b in range(block_ref.shape[0])]
    return jnp.concatenate(picks, axis=1)


def pick(want, block_ref, first_ref, second_ref):
    hot, half = hot_rows(want, block_ref), first_ref.shape[0]
    done = jnp.dot(hot[:, :half], first_ref[...], preferred_element_type=F32)
    return done + jnp.dot(hot[:, half:], second_ref[...], preferred_element_type=F32)


def place_near_kernel(block_ref, want_ref, first_ref, second_ref, out_ref):
    rows = 512

    def step(i, carry):
        spot = pl.ds(pl.multiple_of(i * rows, rows), rows)
        out_ref[spot, :] = pick(want_ref[spot, :], block_ref, first_ref, second_ref).astype(BF)
        return carry

    lax.fori_loop(0, want_ref.shape[0] // rows, step, 0)


def place_far_kernel(block_ref, want_ref, first_ref, second_ref, near_ref, q_ref, kv_ref, before_ref, sems):
    rows = 512
    steps = want_ref.shape[0] // rows
    copies = [
        pltpu.make_async_copy(near_ref.at[pl.ds(i * rows, rows)], before_ref.at[pl.ds(i * rows, rows)], sems.at[i])
        for i in range(steps)
    ]
    for copy in copies:
        copy.start()
    for i, copy in enumerate(copies):
        spot = slice(i * rows, (i + 1) * rows)
        done = pick(want_ref[spot, :], block_ref, first_ref, second_ref)
        copy.wait()
        done = done + before_ref[spot, :].astype(F32)
        q_ref[spot, :] = done[:, :TILE].astype(BF)
        kv_ref[spot, TILE:] = done[:, 2 * TILE :].astype(BF)
        for t in range(0, rows, TILE):
            keys = done[t : t + TILE, TILE : 2 * TILE]
            kv_ref[i * rows + t : i * rows + t + TILE, :TILE] = keys.T.astype(BF)


def place_near(blocks, want, first, second):
    n, width = want.shape[0], first.shape[1]
    return pl.pallas_call(
        place_near_kernel,
        out_shape=jax.ShapeDtypeStruct((n, width), BF),
        in_specs=[WHOLE_SM] + [WHOLE_VM] * 3,
        out_specs=WHOLE_VM,
        compiler_params=pltpu.CompilerParams(vmem_limit_bytes=24 << 20),
        cost_estimate=pl.CostEstimate(flops=n * n * width, bytes_accessed=4 << 20, transcendentals=0),
    )(blocks, want, first, second)


def place_far(blocks, want, first, second, near):
    n, width = want.shape[0], first.shape[1]
    return pl.pallas_call(
        place_far_kernel,
        out_shape=(pltpu.HBM((n, TILE), BF), jax.ShapeDtypeStruct((n, width - TILE), BF)),
        in_specs=[WHOLE_SM] + [WHOLE_VM] * 3 + [WHOLE_ANY],
        out_specs=(WHOLE_VM,) * 2,
        scratch_shapes=[VM((n, width), BF), pltpu.SemaphoreType.DMA((4,))],
        compiler_params=pltpu.CompilerParams(vmem_limit_bytes=24 << 20),
        cost_estimate=pl.CostEstimate(flops=n * n * width, bytes_accessed=4 << 20, transcendentals=0),
    )(blocks, want, first, second, *in_hbm((near,)))


def attend_kernel(sizes, together, parts, last, index_ref, count_ref, q_ref, *refs):
    frames = refs[:parts]
    refs = refs[parts:]
    if last:
        old_ref, stat_ref, out_ref = refs[:3]
    else:
        out_ref, stat_ref = refs[:2]
    win_ref, score_ref, sems = refs[-3:]
    copies, start = [], 0
    for i, frame in enumerate(frames):
        copies.append(pltpu.make_async_copy(frame, win_ref.at[pl.ds(start, frame.shape[0])], sems.at[i]))
        start += frame.shape[0]
    for copy in copies:
        copy.start()
    for copy in copies:
        copy.wait()
    scale = LOG2E / math.sqrt(TILE)

    ones = jnp.ones((2 * TILE, TILE), BF)
    none = jnp.zeros((TILE, TILE), BF)

    def look(t, u, slots):
        q = q_ref[pl.ds(pl.multiple_of(t * TILE, TILE), TILE), :]
        top = None
        for j in range(0, slots, 2):
            spots = [pl.multiple_of(index_ref[t, j + h] * TILE, TILE) for h in range(2)]
            k = jnp.concatenate([win_ref[pl.ds(s, TILE), :TILE] for s in spots], axis=1)
            s = jnp.dot(q, k, preferred_element_type=F32)
            score_ref[u, j // 2] = s
            s = jnp.maximum(s[:, :TILE], s[:, TILE:])
            top = s if top is None else jnp.maximum(top, s)
        return jnp.max(top, axis=1, keepdims=True) * scale

    def weigh(t, u, slots, peak):
        base = pl.multiple_of(t * TILE, TILE)
        count = count_ref[t]
        if last:
            old = stat_ref[pl.ds(base, TILE), :]
            before = old[:, 0:1]
            peak = jnp.where(count > 0, jnp.maximum(peak, before), before)
        done = None
        for j in range(0, slots, 2):
            spots = [pl.multiple_of(index_ref[t, j + h] * TILE, TILE) for h in range(2)]
            e = jnp.exp2(score_ref[u, j // 2] * scale - peak).astype(BF)
            e = jnp.concatenate([jnp.where(j + h < count, e[:, h * TILE : (h + 1) * TILE], none) for h in range(2)], axis=1)
            v = jnp.concatenate([win_ref[pl.ds(s, TILE), TILE:] for s in spots], axis=0)
            part = jnp.dot(e, jnp.concatenate([v, ones], axis=1), preferred_element_type=F32)
            done = part if done is None else done + part
        value, total = done[:, :TILE], done[:, TILE:]
        if last:
            shrink = jnp.exp2(before - peak)
            total = total + shrink * old[:, 1:2]
            value = value + shrink * old_ref[pl.ds(base, TILE), :]
            out_ref[pl.ds(base, TILE), :] = (value / total).astype(BF)
        else:
            peak = jnp.where(count > 0, peak, -1e30)
            out_ref[pl.ds(base, TILE), :] = value
            lane = lax.broadcasted_iota(jnp.int32, (TILE, TILE), 1)
            stat_ref[pl.ds(base, TILE), :] = jnp.where(lane == 0, peak, total)

    def step(i, carry):
        tiles = [i * together + u for u in range(together)]
        most = functools.reduce(jnp.maximum, [count_ref[t] for t in tiles])
        for k, slots in enumerate(sizes):
            fits = most <= slots
            if k > 0:
                fits = jnp.logical_and(fits, most > sizes[k - 1])

            @pl.when(fits)
            def _(slots=slots):
                peaks = [look(t, u, slots) for u, t in enumerate(tiles)]
                for u, t in enumerate(tiles):
                    weigh(t, u, slots, peaks[u])

        return carry

    lax.fori_loop(0, q_ref.shape[0] // TILE // together, step, 0)


def attend(index, count, q, frames, sizes, old=None, together=2):
    n, slots = q.shape[0], index.shape[1]
    rows = sum(f.shape[0] for f in frames)
    wide = jax.ShapeDtypeStruct((n, TILE), F32)
    return pl.pallas_call(
        functools.partial(attend_kernel, sizes, together, len(frames), old is not None),
        out_shape=(wide, wide) if old is None else jax.ShapeDtypeStruct((n, TILE), BF),
        in_specs=[WHOLE_SM] * 2 + [WHOLE_VM] + [WHOLE_ANY] * len(frames) + [WHOLE_VM] * (0 if old is None else 2),
        out_specs=(WHOLE_VM,) * 2 if old is None else WHOLE_VM,
        scratch_shapes=[
            VM((rows, 2 * TILE), BF),
            VM((together, sizes[-1] // 2, TILE, 2 * TILE), F32),
            pltpu.SemaphoreType.DMA((len(frames),)),
        ],
        compiler_params=pltpu.CompilerParams(vmem_limit_bytes=24 << 20),
        cost_estimate=pl.CostEstimate(
            flops=4 * 4 * n * slots * TILE * TILE, bytes_accessed=6 << 20, transcendentals=n * slots * TILE
        ),
    )(index, count, q, *frames, *(old or ()))


def project_kernel(order_ref, att_ref, *refs):
    weights, (mine_ref, other_ref, w_ref, sems) = refs[:-4], refs[-4:]
    chips, width, groups = att_ref.shape[0], mine_ref.shape[1], 3
    span = width // groups
    loads = []
    for g in range(groups):
        for b, ref in enumerate(weights):
            columns = slice(g * span, (g + 1) * span)
            loads.append(
                pltpu.make_async_copy(ref.at[:, columns], w_ref.at[pl.ds(b * TILE, TILE), columns], sems.at[g * chips + b])
            )
    for copy in loads:
        copy.start()
    own = pl.multiple_of(order_ref[chips] * TILE, TILE)
    away = pl.multiple_of(TILE - own, TILE)
    mine = jnp.concatenate([att_ref[order_ref[b], pl.ds(own, TILE), :] for b in range(chips)], axis=1)
    other = jnp.concatenate([att_ref[order_ref[b], pl.ds(away, TILE), :] for b in range(chips)], axis=1)
    left = jnp.concatenate([mine, other], axis=0)
    for g in range(groups):
        for copy in loads[g * chips : (g + 1) * chips]:
            copy.wait()
        for column in range(g * span, (g + 1) * span, 256):
            done = jnp.dot(left, w_ref[:, column : column + 256], preferred_element_type=F32)
            mine_ref[:, column : column + 256] = done[:TILE]
            other_ref[:, column : column + 256] = done[TILE:].astype(BF)


def project(order, attended, weights):
    width, chips = weights[0].shape[1], len(weights)
    return pl.pallas_call(
        project_kernel,
        out_shape=(jax.ShapeDtypeStruct((TILE, width), F32), jax.ShapeDtypeStruct((TILE, width), BF)),
        in_specs=[WHOLE_SM, WHOLE_VM] + [WHOLE_HBM] * chips,
        out_specs=(WHOLE_VM,) * 2,
        scratch_shapes=[VM((chips * TILE, width), BF), pltpu.SemaphoreType.DMA((3 * chips,))],
        compiler_params=pltpu.CompilerParams(vmem_limit_bytes=24 << 20),
        cost_estimate=pl.CostEstimate(flops=4 * TILE * 8 * TILE * width, bytes_accessed=10 << 20, transcendentals=0),
    )(order, attended, *in_hbm(weights))


def listed(place, chosen, slots):
    before = jnp.arange(place.shape[1])[None, :] < jnp.arange(place.shape[1])[:, None]
    rank = jnp.sum(jnp.where(before[None] & chosen[:, None, :], 1, 0), axis=2)
    count = jnp.sum(chosen.astype(jnp.int32), axis=1)
    lead = jnp.minimum(jnp.arange(slots)[None, :], jnp.maximum(count - 1, 0)[:, None])
    lead = jnp.where(jnp.arange(slots)[None, :] < count[:, None], lead, 0)
    hit = (rank[:, None, :] == lead[:, :, None]) & chosen[:, None, :]
    return jnp.sum(jnp.where(hit, place[:, None, :], 0), axis=2).astype(jnp.int32), count


def body(tokens, w_qkv, w_out, source_row, key_tiles, key_count):
    z, yl = lax.axis_index("z"), lax.axis_index("yl")
    yh, x, core = lax.axis_index("yh"), lax.axis_index("x"), lax.axis_index("core")
    after = lax.optimization_barrier

    def chips(part):
        return [((yh + dy) % 2) * 4 + (x + 4 - dx) % 4 for dy, dx in part]

    def blocks(part):
        return jnp.stack([2 * c + side for side in (core, 1 - core) for c in chips(part)]).astype(F32)

    one, three = round_x(tokens, 1), round_x(tokens, -1)
    far_own = swap(tokens, "yh")
    w_other = swap(w_qkv, "core")
    half = tokens.shape[0] // 2
    low, high = round_x(one[:half], 1), round_x(three[half:], -1)
    far_next, _ = after((far_own, (one, three)))
    f_one, f_three = round_x(far_next, 1), round_x(far_next, -1)
    far_two = swap(jnp.concatenate([low, high], axis=0), "yh")
    near_mine, near_theirs = qkv(w_qkv, w_other, [tokens, one, three, far_own])
    near_other = swap(near_theirs, "core")
    want = source_row[0][:, None]
    near = place_near(blocks(NEAR), want, near_mine, near_other)
    tiles, slots = key_tiles.shape
    relative = key_tiles - ((z * 2 + yl) - 2) * tiles
    frame, inside = relative // tiles, relative % tiles
    crossing = frame == jnp.where(yl == 0, 1, 3)
    window = jnp.where(frame == 2, 0, jnp.where(frame == 0, 1, jnp.where(frame == 4, 3, 2)))
    valid = jnp.arange(slots)[None, :] < key_count[:, None]
    index, count = listed(window * tiles + inside, valid & ~crossing, slots)
    cross_index, cross_count = listed(inside, valid & crossing, tiles)
    lists = (index, count, cross_index, cross_count)
    far_two, near, (index, count, cross_index, cross_count) = after((far_two, near, lists))
    far_mine, far_theirs = qkv(w_qkv, w_other, [low, high, f_one, f_three, far_two])
    far_other = swap(far_theirs, "core")

    w_start, _ = after((w_out, near))
    w_one, w_three = round_x(w_start, 1), round_x(w_start, -1)
    w_turn, _ = after((w_out, far_two))
    w_two, w_far = round_x(w_turn, 2), opposite(w_turn)

    q, kv = place_far(blocks(FAR), want, far_mine, far_other, near)
    kv, _ = after((kv, (w_one, w_three)))
    behind = lax.ppermute(kv, "z", [(i, (i + 1) % 8) for i in range(8)])
    ahead = lax.ppermute(kv, "z", [(i, (i + 7) % 8) for i in range(8)])
    beside = swap(kv, "yl")

    wf_one, wf_three, wf_two = opposite(w_one), opposite(w_three), round_x(w_far, 2)

    mid = kv.shape[0] // 2
    (ahead_low, behind_low), _ = after(((ahead[:mid], behind[:mid]), (w_two, w_far)))
    cross_low = swap(jnp.where(yl == 0, ahead_low, behind_low), "yl")
    onward = [(2 * i, 2 * ((i + 1) % 8)) for i in range(8)] + [(2 * i + 1, 2 * ((i + 7) % 8) + 1) for i in range(8)]
    cross_high = lax.ppermute(beside[mid:], CTX, onward)

    state = attend(index, count, q, [kv, behind, beside, ahead], (24, slots), together=4)
    attended = attend(cross_index, cross_count, q, [cross_low, cross_high], (6, tiles), state, together=4)

    pieces = lax.all_to_all(attended.reshape(8, 2 * TILE, TILE), CHIPS, split_axis=0, concat_axis=0, tiled=True)
    order = jnp.stack(chips(((0, 0), (0, 1), (0, 3), (0, 2), (1, 0), (1, 1), (1, 3), (1, 2))) + [core]).astype(jnp.int32)
    weights = [w_out, w_one, w_three, w_two, w_far, wf_one, wf_three, wf_two]
    mine, other = project(order, pieces, weights)
    return (mine + swap(other, "core").astype(F32)).astype(BF)


def solution(mesh):
    fine = Mesh(mesh.devices.reshape(8, 2, 2, 4, 2), ALL)
    in_specs = (
        P(ALL, None),
        P(None, ("yh", "x", "core")),
        P(("yh", "x", "core"), None),
        P(CTX, None),
        P(CTX, None),
        P(CTX),
    )
    return jax.shard_map(body, mesh=fine, in_specs=in_specs, out_specs=P(ALL, None), check_vma=False)
```

```python
import functools
import math

import jax
import jax.numpy as jnp
from jax import lax
from jax.experimental import pallas as pl
from jax.experimental.pallas import tpu as pltpu
from jax.sharding import Mesh
from jax.sharding import PartitionSpec as P

BF = jnp.bfloat16
F32 = jnp.float32
TILE = 128
LOG2E = 1.4426950408889634
VM = pltpu.VMEM
SM = pltpu.SMEM
CTX = ("z", "yl")
CHIPS = ("yh", "x")
ALL = ("z", "yl", "yh", "x", "core")
NEAR = ((0, 0), (0, 1), (0, 3), (1, 0))
FAR = ((0, 2), (1, 1), (1, 3), (1, 2))
WHOLE_VM = pl.BlockSpec(memory_space=VM)
WHOLE_SM = pl.BlockSpec(memory_space=SM)
WHOLE_ANY = pl.BlockSpec(memory_space=pl.ANY)
WHOLE_HBM = pl.BlockSpec(memory_space=pltpu.HBM)


def in_hbm(arrays):
    return [pltpu.with_memory_space_constraint(a, pltpu.HBM) for a in arrays]


def round_x(array, by):
    return lax.ppermute(array, "x", [(i, (i + by) % 4) for i in range(4)])


def swap(array, axis):
    return lax.ppermute(array, axis, [(0, 1), (1, 0)])


def opposite(array):
    return lax.ppermute(array, ("yl", "yh"), [(i, 3 - i) for i in range(4)])


def qkv_kernel(heights, first, chunks, own_ref, other_ref, *refs):
    pieces = refs[: len(heights)]
    mine_ref, theirs_ref, rows_ref, w_ref, sum_ref, sems = refs[len(heights) :]
    width = mine_ref.shape[1]
    span = own_ref.shape[0] // chunks
    loads = []
    for c in range(chunks):
        depth = pl.ds(c * span, span)
        group, start = [], 0
        for side, ref in enumerate((other_ref, own_ref)):
            group.append((ref.at[depth, first : first + width], w_ref.at[depth, side * width : (side + 1) * width]))
        for piece, height in zip(pieces, heights):
            group.append((piece.at[:, depth], rows_ref.at[pl.ds(start, height), depth]))
            start += height
        loads.append([pltpu.make_async_copy(a, b, sems.at[c, i]) for i, (a, b) in enumerate(group)])
    for group in loads:
        for copy in group:
            copy.start()
    for c, group in enumerate(loads):
        for copy in group:
            copy.wait()
        depth = slice(c * span, (c + 1) * span)
        done = jnp.dot(rows_ref[:, depth], w_ref[depth, :], preferred_element_type=F32)
        if c > 0:
            done = done + sum_ref[...]
        if c < chunks - 1:
            sum_ref[...] = done
    theirs_ref[...] = done[:, :width].astype(BF)
    mine_ref[...] = done[:, width:].astype(BF)


def qkv(own, other, pieces, first, last):
    heights, chunks = tuple(p.shape[0] for p in pieces), 3
    n, depth, width = sum(heights), own.shape[0], last - first
    return pl.pallas_call(
        functools.partial(qkv_kernel, heights, first, chunks),
        out_shape=(jax.ShapeDtypeStruct((n, width), BF),) * 2,
        in_specs=[WHOLE_HBM] * 2 + [WHOLE_ANY] * len(pieces),
        out_specs=(WHOLE_VM,) * 2,
        scratch_shapes=[
            VM((n, depth), BF),
            VM((depth, 2 * width), BF),
            VM((n, 2 * width), F32),
            pltpu.SemaphoreType.DMA((chunks, 2 + len(pieces))),
        ],
        compiler_params=pltpu.CompilerParams(vmem_limit_bytes=24 << 20),
        cost_estimate=pl.CostEstimate(flops=4 * n * width, bytes_accessed=1 << 10, transcendentals=0),
    )(*in_hbm((own, other)), *pieces)


def hot_rows(want, block_ref):
    n = want.shape[0]
    want = jnp.broadcast_to(want, (n, TILE))
    high = lax.shift_right_logical(want, 7).astype(F32).astype(BF)
    low = want & (TILE - 1)
    inside = jnp.where(low == lax.broadcasted_iota(jnp.int32, (n, TILE), 1), 1.0, 0.0).astype(BF)
    zero = jnp.zeros((n, TILE), BF)
    picks = [jnp.where(high == block_ref[b].astype(BF), inside, zero) for b in range(block_ref.shape[0])]
    return jnp.concatenate(picks, axis=1)


def pick(want, block_ref, first_ref, second_ref):
    hot, half = hot_rows(want, block_ref), first_ref.shape[0]
    done = jnp.dot(hot[:, :half], first_ref[...], preferred_element_type=F32)
    return done + jnp.dot(hot[:, half:], second_ref[...], preferred_element_type=F32)


def place_near_kernel(block_ref, want_ref, first_ref, second_ref, out_ref):
    rows = 512

    def step(i, carry):
        spot = pl.ds(pl.multiple_of(i * rows, rows), rows)
        out_ref[spot, :] = pick(want_ref[spot, :], block_ref, first_ref, second_ref).astype(BF)
        return carry

    lax.fori_loop(0, want_ref.shape[0] // rows, step, 0)


def place_far_kernel(block_ref, want_ref, first_ref, second_ref, near_ref, q_ref, kv_ref, before_ref, sems):
    rows = 512
    steps = want_ref.shape[0] // rows
    copies = [
        pltpu.make_async_copy(near_ref.at[pl.ds(i * rows, rows)], before_ref.at[pl.ds(i * rows, rows)], sems.at[i])
        for i in range(steps)
    ]
    for copy in copies:
        copy.start()
    for i, copy in enumerate(copies):
        spot = slice(i * rows, (i + 1) * rows)
        done = pick(want_ref[spot, :], block_ref, first_ref, second_ref)
        copy.wait()
        done = done + before_ref[spot, :].astype(F32)
        q_ref[spot, :] = done[:, :TILE].astype(BF)
        kv_ref[spot, TILE:] = done[:, 2 * TILE :].astype(BF)
        for t in range(0, rows, TILE):
            keys = done[t : t + TILE, TILE : 2 * TILE]
            kv_ref[i * rows + t : i * rows + t + TILE, :TILE] = keys.T.astype(BF)


def place_near(blocks, want, first, second):
    n, width = want.shape[0], first.shape[1]
    return pl.pallas_call(
        place_near_kernel,
        out_shape=jax.ShapeDtypeStruct((n, width), BF),
        in_specs=[WHOLE_SM] + [WHOLE_VM] * 3,
        out_specs=WHOLE_VM,
        compiler_params=pltpu.CompilerParams(vmem_limit_bytes=24 << 20),
        cost_estimate=pl.CostEstimate(flops=n * n * width, bytes_accessed=4 << 20, transcendentals=0),
    )(blocks, want, first, second)


def place_far(blocks, want, first, second, near):
    n, width = want.shape[0], first.shape[1]
    return pl.pallas_call(
        place_far_kernel,
        out_shape=(pltpu.HBM((n, TILE), BF), jax.ShapeDtypeStruct((n, width - TILE), BF)),
        in_specs=[WHOLE_SM] + [WHOLE_VM] * 3 + [WHOLE_ANY],
        out_specs=(WHOLE_VM,) * 2,
        scratch_shapes=[VM((n, width), BF), pltpu.SemaphoreType.DMA((4,))],
        compiler_params=pltpu.CompilerParams(vmem_limit_bytes=24 << 20),
        cost_estimate=pl.CostEstimate(flops=n * n * width, bytes_accessed=4 << 20, transcendentals=0),
    )(blocks, want, first, second, *in_hbm((near,)))


def attend_kernel(sizes, together, parts, last, index_ref, count_ref, q_ref, *refs):
    frames = refs[:parts]
    refs = refs[parts:]
    if last:
        old_ref, stat_ref, out_ref = refs[:3]
    else:
        out_ref, stat_ref = refs[:2]
    win_ref, score_ref, sems = refs[-3:]
    copies, start = [], 0
    for i, frame in enumerate(frames):
        copies.append(pltpu.make_async_copy(frame, win_ref.at[pl.ds(start, frame.shape[0])], sems.at[i]))
        start += frame.shape[0]
    for copy in copies:
        copy.start()
    for copy in copies:
        copy.wait()
    scale = LOG2E / math.sqrt(TILE)

    ones = jnp.ones((2 * TILE, TILE), BF)
    none = jnp.zeros((TILE, TILE), BF)

    def look(t, u, slots):
        q = q_ref[pl.ds(pl.multiple_of(t * TILE, TILE), TILE), :]
        top = None
        for j in range(0, slots, 2):
            spots = [pl.multiple_of(index_ref[t, j + h] * TILE, TILE) for h in range(2)]
            k = jnp.concatenate([win_ref[pl.ds(s, TILE), :TILE] for s in spots], axis=1)
            s = jnp.dot(q, k, preferred_element_type=F32)
            score_ref[u, j // 2] = s
            s = jnp.maximum(s[:, :TILE], s[:, TILE:])
            top = s if top is None else jnp.maximum(top, s)
        return jnp.max(top, axis=1, keepdims=True) * scale

    def weigh(t, u, slots, peak):
        base = pl.multiple_of(t * TILE, TILE)
        count = count_ref[t]
        if last:
            old = stat_ref[pl.ds(base, TILE), :]
            before = old[:, 0:1]
            peak = jnp.where(count > 0, jnp.maximum(peak, before), before)
        done = None
        for j in range(0, slots, 2):
            spots = [pl.multiple_of(index_ref[t, j + h] * TILE, TILE) for h in range(2)]
            e = jnp.exp2(score_ref[u, j // 2] * scale - peak).astype(BF)
            e = jnp.concatenate([jnp.where(j + h < count, e[:, h * TILE : (h + 1) * TILE], none) for h in range(2)], axis=1)
            v = jnp.concatenate([win_ref[pl.ds(s, TILE), TILE:] for s in spots], axis=0)
            part = jnp.dot(e, jnp.concatenate([v, ones], axis=1), preferred_element_type=F32)
            done = part if done is None else done + part
        value, total = done[:, :TILE], done[:, TILE:]
        if last:
            shrink = jnp.exp2(before - peak)
            total = total + shrink * old[:, 1:2]
            value = value + shrink * old_ref[pl.ds(base, TILE), :]
            out_ref[pl.ds(base, TILE), :] = (value / total).astype(BF)
        else:
            peak = jnp.where(count > 0, peak, -1e30)
            out_ref[pl.ds(base, TILE), :] = value
            lane = lax.broadcasted_iota(jnp.int32, (TILE, TILE), 1)
            stat_ref[pl.ds(base, TILE), :] = jnp.where(lane == 0, peak, total)

    def step(i, carry):
        tiles = [i * together + u for u in range(together)]
        most = functools.reduce(jnp.maximum, [count_ref[t] for t in tiles])
        for k, slots in enumerate(sizes):
            fits = most <= slots
            if k > 0:
                fits = jnp.logical_and(fits, most > sizes[k - 1])

            @pl.when(fits)
            def _(slots=slots):
                peaks = [look(t, u, slots) for u, t in enumerate(tiles)]
                for u, t in enumerate(tiles):
                    weigh(t, u, slots, peaks[u])

        return carry

    lax.fori_loop(0, q_ref.shape[0] // TILE // together, step, 0)


def attend(index, count, q, frames, sizes, old=None, together=2):
    n, slots = q.shape[0], index.shape[1]
    rows = sum(f.shape[0] for f in frames)
    wide = jax.ShapeDtypeStruct((n, TILE), F32)
    return pl.pallas_call(
        functools.partial(attend_kernel, sizes, together, len(frames), old is not None),
        out_shape=(wide, wide) if old is None else jax.ShapeDtypeStruct((n, TILE), BF),
        in_specs=[WHOLE_SM] * 2 + [WHOLE_VM] + [WHOLE_ANY] * len(frames) + [WHOLE_VM] * (0 if old is None else 2),
        out_specs=(WHOLE_VM,) * 2 if old is None else WHOLE_VM,
        scratch_shapes=[
            VM((rows, 2 * TILE), BF),
            VM((together, sizes[-1] // 2, TILE, 2 * TILE), F32),
            pltpu.SemaphoreType.DMA((len(frames),)),
        ],
        compiler_params=pltpu.CompilerParams(vmem_limit_bytes=24 << 20),
        cost_estimate=pl.CostEstimate(
            flops=4 * 4 * n * slots * TILE * TILE, bytes_accessed=6 << 20, transcendentals=n * slots * TILE
        ),
    )(index, count, q, *frames, *(old or ()))


def project_kernel(order_ref, att_ref, *refs):
    weights, (mine_ref, other_ref, w_ref, sems) = refs[:-4], refs[-4:]
    chips, width, groups = att_ref.shape[0], mine_ref.shape[1], 3
    span = width // groups
    loads = []
    for g in range(groups):
        for b, ref in enumerate(weights):
            columns = slice(g * span, (g + 1) * span)
            loads.append(
                pltpu.make_async_copy(ref.at[:, columns], w_ref.at[pl.ds(b * TILE, TILE), columns], sems.at[g * chips + b])
            )
    for copy in loads:
        copy.start()
    own = pl.multiple_of(order_ref[chips] * TILE, TILE)
    away = pl.multiple_of(TILE - own, TILE)
    mine = jnp.concatenate([att_ref[order_ref[b], pl.ds(own, TILE), :] for b in range(chips)], axis=1)
    other = jnp.concatenate([att_ref[order_ref[b], pl.ds(away, TILE), :] for b in range(chips)], axis=1)
    left = jnp.concatenate([mine, other], axis=0)
    for g in range(groups):
        for copy in loads[g * chips : (g + 1) * chips]:
            copy.wait()
        for column in range(g * span, (g + 1) * span, 256):
            done = jnp.dot(left, w_ref[:, column : column + 256], preferred_element_type=F32)
            mine_ref[:, column : column + 256] = done[:TILE]
            other_ref[:, column : column + 256] = done[TILE:].astype(BF)


def project(order, attended, weights):
    width, chips = weights[0].shape[1], len(weights)
    return pl.pallas_call(
        project_kernel,
        out_shape=(jax.ShapeDtypeStruct((TILE, width), F32), jax.ShapeDtypeStruct((TILE, width), BF)),
        in_specs=[WHOLE_SM, WHOLE_VM] + [WHOLE_HBM] * chips,
        out_specs=(WHOLE_VM,) * 2,
        scratch_shapes=[VM((chips * TILE, width), BF), pltpu.SemaphoreType.DMA((3 * chips,))],
        compiler_params=pltpu.CompilerParams(vmem_limit_bytes=24 << 20),
        cost_estimate=pl.CostEstimate(flops=4 * TILE * 8 * TILE * width, bytes_accessed=10 << 20, transcendentals=0),
    )(order, attended, *in_hbm(weights))


def listed(place, chosen, slots):
    before = jnp.arange(place.shape[1])[None, :] < jnp.arange(place.shape[1])[:, None]
    rank = jnp.sum(jnp.where(before[None] & chosen[:, None, :], 1, 0), axis=2)
    count = jnp.sum(chosen.astype(jnp.int32), axis=1)
    lead = jnp.minimum(jnp.arange(slots)[None, :], jnp.maximum(count - 1, 0)[:, None])
    lead = jnp.where(jnp.arange(slots)[None, :] < count[:, None], lead, 0)
    hit = (rank[:, None, :] == lead[:, :, None]) & chosen[:, None, :]
    return jnp.sum(jnp.where(hit, place[:, None, :], 0), axis=2).astype(jnp.int32), count


def body(tokens, w_qkv, w_out, source_row, key_tiles, key_count):
    z, yl = lax.axis_index("z"), lax.axis_index("yl")
    yh, x, core = lax.axis_index("yh"), lax.axis_index("x"), lax.axis_index("core")
    after = lax.optimization_barrier

    def chips(part):
        return [((yh + dy) % 2) * 4 + (x + 4 - dx) % 4 for dy, dx in part]

    def blocks(part):
        return jnp.stack([2 * c + side for side in (core, 1 - core) for c in chips(part)]).astype(F32)

    one, three = round_x(tokens, 1), round_x(tokens, -1)
    far_own = swap(tokens, "yh")
    w_other = swap(w_qkv, "core")
    half = tokens.shape[0] // 2
    low, high = round_x(one[:half], 1), round_x(three[half:], -1)
    far_next, _ = after((far_own, (one, three)))
    f_one, f_three = round_x(far_next, 1), round_x(far_next, -1)
    far_two = swap(jnp.concatenate([low, high], axis=0), "yh")
    near_mine, near_theirs = qkv(w_qkv, w_other, [tokens, one, three, far_own], 0, 3 * TILE)
    near_other = swap(near_theirs, "core")
    want = source_row[0][:, None]
    near = place_near(blocks(NEAR), want, near_mine, near_other)
    tiles, slots = key_tiles.shape
    relative = key_tiles - ((z * 2 + yl) - 2) * tiles
    frame, inside = relative // tiles, relative % tiles
    crossing = frame == jnp.where(yl == 0, 1, 3)
    window = jnp.where(frame == 2, 0, jnp.where(frame == 0, 1, jnp.where(frame == 4, 3, 2)))
    valid = jnp.arange(slots)[None, :] < key_count[:, None]
    index, count = listed(window * tiles + inside, valid & ~crossing, slots)
    cross_index, cross_count = listed(inside, valid & crossing, tiles)
    lists = (index, count, cross_index, cross_count)
    far_two, near, (index, count, cross_index, cross_count) = after((far_two, near, lists))
    far_mine, far_theirs = qkv(w_qkv, w_other, [low, high, f_one, f_three, far_two], 0, 3 * TILE)
    far_other = swap(far_theirs, "core")

    w_start, _ = after((w_out, near_theirs))
    w_one, w_three = round_x(w_start, 1), round_x(w_start, -1)
    w_turn, _ = after((w_out, far_two))
    w_two, w_far = round_x(w_turn, 2), opposite(w_turn)

    far_other, _ = after((far_other, (w_one, w_three)))
    q, kv = place_far(blocks(FAR), want, far_mine, far_other, near)
    behind = lax.ppermute(kv, "z", [(i, (i + 1) % 8) for i in range(8)])
    ahead = lax.ppermute(kv, "z", [(i, (i + 7) % 8) for i in range(8)])
    beside = swap(kv, "yl")

    mid = kv.shape[0] // 2
    (ahead_low, behind_low), _ = after(((ahead[:mid], behind[:mid]), (w_two, w_far)))
    cross = jnp.where(yl == 0, ahead_low, behind_low)
    cross_low = swap(cross, "yl")
    onward = [(2 * i, 2 * ((i + 1) % 8)) for i in range(8)] + [(2 * i + 1, 2 * ((i + 7) % 8) + 1) for i in range(8)]
    beside_high = beside[mid:]
    cross_high = lax.ppermute(beside_high, CTX, onward)
    (g_one, g_three, g_far), _ = after(((w_one, w_three, w_far), (cross, beside_high)))
    wf_one, wf_three, wf_two = opposite(g_one), opposite(g_three), round_x(g_far, 2)

    state = attend(index, count, q, [kv, behind, beside, ahead], (24, slots), together=4)
    attended = attend(cross_index, cross_count, q, [cross_low, cross_high], (6, tiles), state, together=4)

    pieces = lax.all_to_all(attended.reshape(8, 2 * TILE, TILE), CHIPS, split_axis=0, concat_axis=0, tiled=True)
    order = jnp.stack(chips(((0, 0), (0, 1), (0, 3), (0, 2), (1, 0), (1, 1), (1, 3), (1, 2))) + [core]).astype(jnp.int32)
    weights = [w_out, w_one, w_three, w_two, w_far, wf_one, wf_three, wf_two]
    mine, other = project(order, pieces, weights)
    return (mine + swap(other, "core").astype(F32)).astype(BF)


def solution(mesh):
    fine = Mesh(mesh.devices.reshape(8, 2, 2, 4, 2), ALL)
    in_specs = (
        P(ALL, None),
        P(None, ("yh", "x", "core")),
        P(("yh", "x", "core"), None),
        P(CTX, None),
        P(CTX, None),
        P(CTX),
    )
    return jax.shard_map(body, mesh=fine, in_specs=in_specs, out_specs=P(ALL, None), check_vma=False)
```

```python
import functools
import math

import jax
import jax.numpy as jnp
from jax import lax
from jax.experimental import pallas as pl
from jax.experimental.pallas import tpu as pltpu
from jax.sharding import Mesh
from jax.sharding import PartitionSpec as P

BF = jnp.bfloat16
F32 = jnp.float32
TILE = 128
LOG2E = 1.4426950408889634
VM = pltpu.VMEM
SM = pltpu.SMEM
CTX = ("z", "yl")
CHIPS = ("yh", "x")
ALL = ("z", "yl", "yh", "x", "core")
NEAR = ((0, 0), (0, 1), (0, 3), (1, 0))
FAR = ((0, 2), (1, 1), (1, 3), (1, 2))
WHOLE_VM = pl.BlockSpec(memory_space=VM)
WHOLE_SM = pl.BlockSpec(memory_space=SM)
WHOLE_ANY = pl.BlockSpec(memory_space=pl.ANY)
WHOLE_HBM = pl.BlockSpec(memory_space=pltpu.HBM)


def in_hbm(arrays):
    return [pltpu.with_memory_space_constraint(a, pltpu.HBM) for a in arrays]


def round_x(array, by):
    return lax.ppermute(array, "x", [(i, (i + by) % 4) for i in range(4)])


def swap(array, axis):
    return lax.ppermute(array, axis, [(0, 1), (1, 0)])


def opposite(array):
    return lax.ppermute(array, ("yl", "yh"), [(i, 3 - i) for i in range(4)])


def qkv_kernel(chunks, own_ref, other_ref, *refs):
    pieces, (mine_ref, theirs_ref, w_ref, sum_ref, sems) = refs[:-5], refs[-5:]
    width = mine_ref.shape[1]
    span = own_ref.shape[0] // chunks
    loads = []
    for c in range(chunks):
        depth = pl.ds(c * span, span)
        for side, ref in enumerate((other_ref, own_ref)):
            target = w_ref.at[depth, side * width : (side + 1) * width]
            loads.append(pltpu.make_async_copy(ref.at[depth, :], target, sems.at[2 * c + side]))
    for copy in loads:
        copy.start()
    for c in range(chunks):
        depth = slice(c * span, (c + 1) * span)
        rows = jnp.concatenate([piece[:, depth] for piece in pieces], axis=0)
        loads[2 * c].wait()
        loads[2 * c + 1].wait()
        done = jnp.dot(rows, w_ref[depth, :], preferred_element_type=F32)
        if c > 0:
            done = done + sum_ref[...]
        if c < chunks - 1:
            sum_ref[...] = done
    theirs_ref[...] = done[:, :width].astype(BF)
    mine_ref[...] = done[:, width:].astype(BF)


def qkv(own, other, pieces):
    n, depth, width, chunks = sum(p.shape[0] for p in pieces), own.shape[0], own.shape[1], 3
    return pl.pallas_call(
        functools.partial(qkv_kernel, chunks),
        out_shape=(jax.ShapeDtypeStruct((n, width), BF),) * 2,
        in_specs=[WHOLE_HBM] * 2 + [WHOLE_VM] * len(pieces),
        out_specs=(WHOLE_VM,) * 2,
        scratch_shapes=[
            VM((depth, 2 * width), BF),
            VM((n, 2 * width), F32),
            pltpu.SemaphoreType.DMA((2 * chunks,)),
        ],
        compiler_params=pltpu.CompilerParams(vmem_limit_bytes=24 << 20),
        cost_estimate=pl.CostEstimate(flops=4 * n * depth * width, bytes_accessed=8 << 20, transcendentals=0),
    )(*in_hbm((own, other)), *pieces)


def hot_rows(want, block_ref):
    n = want.shape[0]
    want = jnp.broadcast_to(want, (n, TILE))
    high = lax.shift_right_logical(want, 7).astype(F32).astype(BF)
    low = want & (TILE - 1)
    inside = jnp.where(low == lax.broadcasted_iota(jnp.int32, (n, TILE), 1), 1.0, 0.0).astype(BF)
    zero = jnp.zeros((n, TILE), BF)
    picks = [jnp.where(high == block_ref[b].astype(BF), inside, zero) for b in range(block_ref.shape[0])]
    return jnp.concatenate(picks, axis=1)


def pick(want, block_ref, first_ref, second_ref, columns=slice(None)):
    hot, half = hot_rows(want, block_ref), first_ref.shape[0]
    done = jnp.dot(hot[:, :half], first_ref[:, columns], preferred_element_type=F32)
    return done + jnp.dot(hot[:, half:], second_ref[:, columns], preferred_element_type=F32)


def place_near_kernel(block_ref, want_ref, first_ref, second_ref, out_ref):
    rows = 512

    def step(i, carry):
        spot = pl.ds(pl.multiple_of(i * rows, rows), rows)
        out_ref[spot, :] = pick(want_ref[spot, :], block_ref, first_ref, second_ref).astype(BF)
        return carry

    lax.fori_loop(0, want_ref.shape[0] // rows, step, 0)


def place_far_kernel(column, turn, block_ref, want_ref, first_ref, second_ref, near_ref, out_ref, before_ref, sems):
    rows, width = 512, out_ref.shape[1]
    steps = want_ref.shape[0] // rows
    columns = slice(column, column + width)
    copies = []
    for i in range(steps):
        spot = pl.ds(i * rows, rows)
        copies.append(pltpu.make_async_copy(near_ref.at[spot, columns], before_ref.at[spot], sems.at[i]))
    for copy in copies:
        copy.start()
    for i, copy in enumerate(copies):
        spot = slice(i * rows, (i + 1) * rows)
        done = pick(want_ref[spot, :], block_ref, first_ref, second_ref, columns)
        copy.wait()
        done = done + before_ref[spot, :].astype(F32)
        if not turn:
            out_ref[spot, :] = done.astype(BF)
            continue
        out_ref[spot, TILE:] = done[:, TILE:].astype(BF)
        for t in range(0, rows, TILE):
            out_ref[i * rows + t : i * rows + t + TILE, :TILE] = done[t : t + TILE, :TILE].T.astype(BF)


def place_near(blocks, want, first, second):
    n, width = want.shape[0], first.shape[1]
    return pl.pallas_call(
        place_near_kernel,
        out_shape=jax.ShapeDtypeStruct((n, width), BF),
        in_specs=[WHOLE_SM] + [WHOLE_VM] * 3,
        out_specs=WHOLE_VM,
        compiler_params=pltpu.CompilerParams(vmem_limit_bytes=24 << 20),
        cost_estimate=pl.CostEstimate(flops=n * n * width, bytes_accessed=4 << 20, transcendentals=0),
    )(blocks, want, first, second)


def place_far(blocks, want, first, second, near, column, width, turn):
    n = want.shape[0]
    return pl.pallas_call(
        functools.partial(place_far_kernel, column, turn),
        out_shape=pltpu.HBM((n, width), BF),
        in_specs=[WHOLE_SM] + [WHOLE_VM] * 3 + [WHOLE_HBM],
        out_specs=WHOLE_VM,
        scratch_shapes=[VM((n, width), BF), pltpu.SemaphoreType.DMA((4,))],
        compiler_params=pltpu.CompilerParams(vmem_limit_bytes=24 << 20),
        cost_estimate=pl.CostEstimate(flops=n * n * width, bytes_accessed=4 << 20, transcendentals=0),
    )(blocks, want, first, second, *in_hbm((near,)))


def attend_kernel(sizes, together, parts, last, index_ref, count_ref, q_ref, *refs):
    frames = refs[:parts]
    refs = refs[parts:]
    if last:
        old_ref, stat_ref, out_ref = refs[:3]
    else:
        out_ref, stat_ref = refs[:2]
    win_ref, score_ref, sems = refs[-3:]
    copies, start = [], 0
    for i, frame in enumerate(frames):
        copies.append(pltpu.make_async_copy(frame, win_ref.at[pl.ds(start, frame.shape[0])], sems.at[i]))
        start += frame.shape[0]
    for copy in copies:
        copy.start()
    for copy in copies:
        copy.wait()
    scale = LOG2E / math.sqrt(TILE)

    ones = jnp.ones((2 * TILE, TILE), BF)
    none = jnp.zeros((TILE, TILE), BF)

    def look(t, u, slots):
        q = q_ref[pl.ds(pl.multiple_of(t * TILE, TILE), TILE), :]
        top = None
        for j in range(0, slots, 2):
            spots = [pl.multiple_of(index_ref[t, j + h] * TILE, TILE) for h in range(2)]
            k = jnp.concatenate([win_ref[pl.ds(s, TILE), :TILE] for s in spots], axis=1)
            s = jnp.dot(q, k, preferred_element_type=F32)
            score_ref[u, j // 2] = s
            s = jnp.maximum(s[:, :TILE], s[:, TILE:])
            top = s if top is None else jnp.maximum(top, s)
        return jnp.max(top, axis=1, keepdims=True) * scale

    def weigh(t, u, slots, peak):
        base = pl.multiple_of(t * TILE, TILE)
        count = count_ref[t]
        if last:
            old = stat_ref[pl.ds(base, TILE), :]
            before = old[:, 0:1]
            peak = jnp.where(count > 0, jnp.maximum(peak, before), before)
        done = None
        for j in range(0, slots, 2):
            spots = [pl.multiple_of(index_ref[t, j + h] * TILE, TILE) for h in range(2)]
            e = jnp.exp2(score_ref[u, j // 2] * scale - peak).astype(BF)
            e = jnp.concatenate([jnp.where(j + h < count, e[:, h * TILE : (h + 1) * TILE], none) for h in range(2)], axis=1)
            v = jnp.concatenate([win_ref[pl.ds(s, TILE), TILE:] for s in spots], axis=0)
            part = jnp.dot(e, jnp.concatenate([v, ones], axis=1), preferred_element_type=F32)
            done = part if done is None else done + part
        value, total = done[:, :TILE], done[:, TILE:]
        if last:
            shrink = jnp.exp2(before - peak)
            total = total + shrink * old[:, 1:2]
            value = value + shrink * old_ref[pl.ds(base, TILE), :]
            out_ref[pl.ds(base, TILE), :] = (value / total).astype(BF)
        else:
            peak = jnp.where(count > 0, peak, -1e30)
            out_ref[pl.ds(base, TILE), :] = value
            lane = lax.broadcasted_iota(jnp.int32, (TILE, TILE), 1)
            stat_ref[pl.ds(base, TILE), :] = jnp.where(lane == 0, peak, total)

    def step(i, carry):
        tiles = [i * together + u for u in range(together)]
        most = functools.reduce(jnp.maximum, [count_ref[t] for t in tiles])
        for k, slots in enumerate(sizes):
            fits = most <= slots
            if k > 0:
                fits = jnp.logical_and(fits, most > sizes[k - 1])

            @pl.when(fits)
            def _(slots=slots):
                peaks = [look(t, u, slots) for u, t in enumerate(tiles)]
                for u, t in enumerate(tiles):
                    weigh(t, u, slots, peaks[u])

        return carry

    lax.fori_loop(0, q_ref.shape[0] // TILE // together, step, 0)


def attend(index, count, q, frames, sizes, old=None, together=2):
    n, slots = q.shape[0], index.shape[1]
    rows = sum(f.shape[0] for f in frames)
    wide = jax.ShapeDtypeStruct((n, TILE), F32)
    return pl.pallas_call(
        functools.partial(attend_kernel, sizes, together, len(frames), old is not None),
        out_shape=(wide, wide) if old is None else jax.ShapeDtypeStruct((n, TILE), BF),
        in_specs=[WHOLE_SM] * 2 + [WHOLE_VM] + [WHOLE_ANY] * len(frames) + [WHOLE_VM] * (0 if old is None else 2),
        out_specs=(WHOLE_VM,) * 2 if old is None else WHOLE_VM,
        scratch_shapes=[
            VM((rows, 2 * TILE), BF),
            VM((together, sizes[-1] // 2, TILE, 2 * TILE), F32),
            pltpu.SemaphoreType.DMA((len(frames),)),
        ],
        compiler_params=pltpu.CompilerParams(vmem_limit_bytes=24 << 20),
        cost_estimate=pl.CostEstimate(
            flops=4 * 4 * n * slots * TILE * TILE, bytes_accessed=6 << 20, transcendentals=n * slots * TILE
        ),
    )(index, count, q, *frames, *(old or ()))


def project_kernel(order_ref, att_ref, *refs):
    weights, (mine_ref, other_ref, w_ref, sems) = refs[:-4], refs[-4:]
    chips, width, groups = att_ref.shape[0], mine_ref.shape[1], 3
    span = width // groups
    loads = []
    for g in range(groups):
        for b, ref in enumerate(weights):
            columns = slice(g * span, (g + 1) * span)
            loads.append(
                pltpu.make_async_copy(ref.at[:, columns], w_ref.at[pl.ds(b * TILE, TILE), columns], sems.at[g * chips + b])
            )
    for copy in loads:
        copy.start()
    own = pl.multiple_of(order_ref[chips] * TILE, TILE)
    away = pl.multiple_of(TILE - own, TILE)
    mine = jnp.concatenate([att_ref[order_ref[b], pl.ds(own, TILE), :] for b in range(chips)], axis=1)
    other = jnp.concatenate([att_ref[order_ref[b], pl.ds(away, TILE), :] for b in range(chips)], axis=1)
    left = jnp.concatenate([mine, other], axis=0)
    for g in range(groups):
        for copy in loads[g * chips : (g + 1) * chips]:
            copy.wait()
        for column in range(g * span, (g + 1) * span, 256):
            done = jnp.dot(left, w_ref[:, column : column + 256], preferred_element_type=F32)
            mine_ref[:, column : column + 256] = done[:TILE]
            other_ref[:, column : column + 256] = done[TILE:].astype(BF)


def project(order, attended, weights):
    width, chips = weights[0].shape[1], len(weights)
    return pl.pallas_call(
        project_kernel,
        out_shape=(jax.ShapeDtypeStruct((TILE, width), F32), jax.ShapeDtypeStruct((TILE, width), BF)),
        in_specs=[WHOLE_SM, WHOLE_VM] + [WHOLE_HBM] * chips,
        out_specs=(WHOLE_VM,) * 2,
        scratch_shapes=[VM((chips * TILE, width), BF), pltpu.SemaphoreType.DMA((3 * chips,))],
        compiler_params=pltpu.CompilerParams(vmem_limit_bytes=24 << 20),
        cost_estimate=pl.CostEstimate(flops=4 * TILE * 8 * TILE * width, bytes_accessed=10 << 20, transcendentals=0),
    )(order, attended, *in_hbm(weights))


def listed(place, chosen, slots):
    before = jnp.arange(place.shape[1])[None, :] < jnp.arange(place.shape[1])[:, None]
    rank = jnp.sum(jnp.where(before[None] & chosen[:, None, :], 1, 0), axis=2)
    count = jnp.sum(chosen.astype(jnp.int32), axis=1)
    lead = jnp.minimum(jnp.arange(slots)[None, :], jnp.maximum(count - 1, 0)[:, None])
    lead = jnp.where(jnp.arange(slots)[None, :] < count[:, None], lead, 0)
    hit = (rank[:, None, :] == lead[:, :, None]) & chosen[:, None, :]
    return jnp.sum(jnp.where(hit, place[:, None, :], 0), axis=2).astype(jnp.int32), count


def body(tokens, w_qkv, w_out, source_row, key_tiles, key_count):
    z, yl = lax.axis_index("z"), lax.axis_index("yl")
    yh, x, core = lax.axis_index("yh"), lax.axis_index("x"), lax.axis_index("core")
    after = lax.optimization_barrier

    def chips(part):
        return [((yh + dy) % 2) * 4 + (x + 4 - dx) % 4 for dy, dx in part]

    def blocks(part):
        return jnp.stack([2 * c + side for side in (core, 1 - core) for c in chips(part)]).astype(F32)

    one, three = round_x(tokens, 1), round_x(tokens, -1)
    far_own = swap(tokens, "yh")
    w_other = swap(w_qkv, "core")
    half = tokens.shape[0] // 2
    low, high = round_x(one[:half], 1), round_x(three[half:], -1)
    far_next, _ = after((far_own, (one, three)))
    f_one, f_three = round_x(far_next, 1), round_x(far_next, -1)
    far_two = swap(jnp.concatenate([low, high], axis=0), "yh")
    near_mine, near_theirs = qkv(w_qkv, w_other, [tokens, one, three, far_own])
    near_other = swap(near_theirs, "core")
    want = source_row[0][:, None]
    near = place_near(blocks(NEAR), want, near_mine, near_other)
    tiles, slots = key_tiles.shape
    relative = key_tiles - ((z * 2 + yl) - 2) * tiles
    frame, inside = relative // tiles, relative % tiles
    crossing = frame == jnp.where(yl == 0, 1, 3)
    window = jnp.where(frame == 2, 0, jnp.where(frame == 0, 1, jnp.where(frame == 4, 3, 2)))
    valid = jnp.arange(slots)[None, :] < key_count[:, None]
    index, count = listed(window * tiles + inside, valid & ~crossing, slots)
    cross_index, cross_count = listed(inside, valid & crossing, tiles)
    lists = (index, count, cross_index, cross_count)
    far_two, near, (index, count, cross_index, cross_count) = after((far_two, near, lists))
    far_mine, far_theirs = qkv(w_qkv, w_other, [low, high, f_one, f_three, far_two])
    far_other = swap(far_theirs, "core")

    w_start, _ = after((w_out, near))
    w_one, w_three = round_x(w_start, 1), round_x(w_start, -1)
    w_turn, _ = after((w_out, far_two))
    w_two, w_far = round_x(w_turn, 2), opposite(w_turn)

    kv = place_far(blocks(FAR), want, far_mine, far_other, near, TILE, 2 * TILE, True)
    (far_mine, far_other), _ = after(((far_mine, far_other), kv))
    q = place_far(blocks(FAR), want, far_mine, far_other, near, 0, TILE, False)
    kv, _ = after((kv, (w_one, w_three)))
    behind = lax.ppermute(kv, "z", [(i, (i + 1) % 8) for i in range(8)])
    ahead = lax.ppermute(kv, "z", [(i, (i + 7) % 8) for i in range(8)])
    beside = swap(kv, "yl")

    wf_one, wf_three, wf_two = opposite(w_one), opposite(w_three), round_x(w_far, 2)

    mid = kv.shape[0] // 2
    (ahead_low, behind_low), _ = after(((ahead[:mid], behind[:mid]), (w_two, w_far, q)))
    cross_low = swap(jnp.where(yl == 0, ahead_low, behind_low), "yl")
    onward = [(2 * i, 2 * ((i + 1) % 8)) for i in range(8)] + [(2 * i + 1, 2 * ((i + 7) % 8) + 1) for i in range(8)]
    cross_high = lax.ppermute(beside[mid:], CTX, onward)

    state = attend(index, count, q, [kv, behind, beside, ahead], (24, slots), together=4)
    attended = attend(cross_index, cross_count, q, [cross_low, cross_high], (6, tiles), state, together=4)

    pieces = lax.all_to_all(attended.reshape(8, 2 * TILE, TILE), CHIPS, split_axis=0, concat_axis=0, tiled=True)
    order = jnp.stack(chips(((0, 0), (0, 1), (0, 3), (0, 2), (1, 0), (1, 1), (1, 3), (1, 2))) + [core]).astype(jnp.int32)
    weights = [w_out, w_one, w_three, w_two, w_far, wf_one, wf_three, wf_two]
    mine, other = project(order, pieces, weights)
    return (mine + swap(other, "core").astype(F32)).astype(BF)


def solution(mesh):
    fine = Mesh(mesh.devices.reshape(8, 2, 2, 4, 2), ALL)
    in_specs = (
        P(ALL, None),
        P(None, ("yh", "x", "core")),
        P(("yh", "x", "core"), None),
        P(CTX, None),
        P(CTX, None),
        P(CTX),
    )
    return jax.shard_map(body, mesh=fine, in_specs=in_specs, out_specs=P(ALL, None), check_vma=False)
```

```python
import functools
import math

import jax
import jax.numpy as jnp
from jax import lax
from jax.experimental import pallas as pl
from jax.experimental.pallas import tpu as pltpu
from jax.sharding import Mesh
from jax.sharding import PartitionSpec as P

BF = jnp.bfloat16
F32 = jnp.float32
TILE = 128
LOG2E = 1.4426950408889634
VM = pltpu.VMEM
SM = pltpu.SMEM
CTX = ("z", "yl")
CHIPS = ("yh", "x")
ALL = ("z", "yl", "yh", "x", "core")
NEAR = ((0, 0), (0, 1), (0, 3), (1, 0))
FAR = ((0, 2), (1, 1), (1, 3), (1, 2))
WHOLE_VM = pl.BlockSpec(memory_space=VM)
WHOLE_SM = pl.BlockSpec(memory_space=SM)
WHOLE_ANY = pl.BlockSpec(memory_space=pl.ANY)
WHOLE_HBM = pl.BlockSpec(memory_space=pltpu.HBM)


def in_hbm(arrays):
    return [pltpu.with_memory_space_constraint(a, pltpu.HBM) for a in arrays]


def round_x(array, by):
    return lax.ppermute(array, "x", [(i, (i + by) % 4) for i in range(4)])


def swap(array, axis):
    return lax.ppermute(array, axis, [(0, 1), (1, 0)])


def opposite(array):
    return lax.ppermute(array, ("yl", "yh"), [(i, 3 - i) for i in range(4)])


def qkv_kernel(chunks, own_ref, other_ref, *refs):
    pieces, (mine_ref, theirs_ref, w_ref, sum_ref, sems) = refs[:-5], refs[-5:]
    width = mine_ref.shape[1]
    span = own_ref.shape[0] // chunks
    loads = []
    for c in range(chunks):
        depth = pl.ds(c * span, span)
        for side, ref in enumerate((other_ref, own_ref)):
            target = w_ref.at[depth, side * width : (side + 1) * width]
            loads.append(pltpu.make_async_copy(ref.at[depth, :], target, sems.at[2 * c + side]))
    for copy in loads:
        copy.start()
    for c in range(chunks):
        depth = slice(c * span, (c + 1) * span)
        rows = jnp.concatenate([piece[:, depth] for piece in pieces], axis=0)
        loads[2 * c].wait()
        loads[2 * c + 1].wait()
        done = jnp.dot(rows, w_ref[depth, :], preferred_element_type=F32)
        if c > 0:
            done = done + sum_ref[...]
        if c < chunks - 1:
            sum_ref[...] = done
    theirs_ref[...] = done[:, :width].astype(BF)
    mine_ref[...] = done[:, width:].astype(BF)


def qkv(own, other, pieces):
    n, depth, width, chunks = sum(p.shape[0] for p in pieces), own.shape[0], own.shape[1], 3
    return pl.pallas_call(
        functools.partial(qkv_kernel, chunks),
        out_shape=(jax.ShapeDtypeStruct((n, width), BF),) * 2,
        in_specs=[WHOLE_HBM] * 2 + [WHOLE_VM] * len(pieces),
        out_specs=(WHOLE_VM,) * 2,
        scratch_shapes=[
            VM((depth, 2 * width), BF),
            VM((n, 2 * width), F32),
            pltpu.SemaphoreType.DMA((2 * chunks,)),
        ],
        compiler_params=pltpu.CompilerParams(vmem_limit_bytes=24 << 20),
        cost_estimate=pl.CostEstimate(flops=4 * n * depth * width, bytes_accessed=8 << 20, transcendentals=0),
    )(*in_hbm((own, other)), *pieces)


def hot_rows(want, block_ref):
    n = want.shape[0]
    want = jnp.broadcast_to(want, (n, TILE))
    high = lax.shift_right_logical(want, 7).astype(F32).astype(BF)
    low = want & (TILE - 1)
    inside = jnp.where(low == lax.broadcasted_iota(jnp.int32, (n, TILE), 1), 1.0, 0.0).astype(BF)
    zero = jnp.zeros((n, TILE), BF)
    picks = [jnp.where(high == block_ref[b].astype(BF), inside, zero) for b in range(block_ref.shape[0])]
    return jnp.concatenate(picks, axis=1)


def pick(want, block_ref, first_ref, second_ref, columns=slice(None)):
    hot, half = hot_rows(want, block_ref), first_ref.shape[0]
    done = jnp.dot(hot[:, :half], first_ref[:, columns], preferred_element_type=F32)
    return done + jnp.dot(hot[:, half:], second_ref[:, columns], preferred_element_type=F32)


def place_near_kernel(block_ref, want_ref, first_ref, second_ref, out_ref):
    rows = 512

    def step(i, carry):
        spot = pl.ds(pl.multiple_of(i * rows, rows), rows)
        out_ref[spot, :] = pick(want_ref[spot, :], block_ref, first_ref, second_ref).astype(BF)
        return carry

    lax.fori_loop(0, want_ref.shape[0] // rows, step, 0)


def place_far_kernel(block_ref, want_ref, first_ref, second_ref, near_ref, q_ref, kv_ref, before_ref, sems):
    rows = 512
    steps = want_ref.shape[0] // rows
    copies = [
        pltpu.make_async_copy(near_ref.at[pl.ds(i * rows, rows)], before_ref.at[pl.ds(i * rows, rows)], sems.at[i])
        for i in range(steps)
    ]
    for copy in copies:
        copy.start()
    for i, copy in enumerate(copies):
        spot = slice(i * rows, (i + 1) * rows)
        done = pick(want_ref[spot, :], block_ref, first_ref, second_ref)
        copy.wait()
        done = done + before_ref[spot, :].astype(F32)
        q_ref[spot, :] = done[:, :TILE].astype(BF)
        kv_ref[spot, TILE:] = done[:, 2 * TILE :].astype(BF)
        for t in range(0, rows, TILE):
            keys = done[t : t + TILE, TILE : 2 * TILE]
            kv_ref[i * rows + t : i * rows + t + TILE, :TILE] = keys.T.astype(BF)


def place_near(blocks, want, first, second):
    n, width = want.shape[0], first.shape[1]
    return pl.pallas_call(
        place_near_kernel,
        out_shape=jax.ShapeDtypeStruct((n, width), BF),
        in_specs=[WHOLE_SM] + [WHOLE_VM] * 3,
        out_specs=WHOLE_VM,
        compiler_params=pltpu.CompilerParams(vmem_limit_bytes=24 << 20),
        cost_estimate=pl.CostEstimate(flops=n * n * width, bytes_accessed=4 << 20, transcendentals=0),
    )(blocks, want, first, second)


def place_far(blocks, want, first, second, near):
    n, width = want.shape[0], first.shape[1]
    return pl.pallas_call(
        place_far_kernel,
        out_shape=(pltpu.HBM((n, TILE), BF), jax.ShapeDtypeStruct((n, width - TILE), BF)),
        in_specs=[WHOLE_SM] + [WHOLE_VM] * 3 + [WHOLE_ANY],
        out_specs=(WHOLE_VM,) * 2,
        scratch_shapes=[VM((n, width), BF), pltpu.SemaphoreType.DMA((4,))],
        compiler_params=pltpu.CompilerParams(vmem_limit_bytes=24 << 20),
        cost_estimate=pl.CostEstimate(flops=n * n * width, bytes_accessed=4 << 20, transcendentals=0),
    )(blocks, want, first, second, *in_hbm((near,)))


def attend_kernel(sizes, together, parts, last, index_ref, count_ref, q_ref, *refs):
    frames = refs[:parts]
    refs = refs[parts:]
    if last:
        old_ref, stat_ref, out_ref = refs[:3]
    else:
        out_ref, stat_ref = refs[:2]
    win_ref, score_ref, sems = refs[-3:]
    copies, start = [], 0
    for i, frame in enumerate(frames):
        copies.append(pltpu.make_async_copy(frame, win_ref.at[pl.ds(start, frame.shape[0])], sems.at[i]))
        start += frame.shape[0]
    for copy in copies:
        copy.start()
    for copy in copies:
        copy.wait()
    scale = LOG2E / math.sqrt(TILE)

    ones = jnp.ones((2 * TILE, TILE), BF)
    none = jnp.zeros((TILE, TILE), BF)

    def look(t, u, slots):
        q = q_ref[pl.ds(pl.multiple_of(t * TILE, TILE), TILE), :]
        top = None
        for j in range(0, slots, 2):
            spots = [pl.multiple_of(index_ref[t, j + h] * TILE, TILE) for h in range(2)]
            k = jnp.concatenate([win_ref[pl.ds(s, TILE), :TILE] for s in spots], axis=1)
            s = jnp.dot(q, k, preferred_element_type=F32)
            score_ref[u, j // 2] = s
            s = jnp.maximum(s[:, :TILE], s[:, TILE:])
            top = s if top is None else jnp.maximum(top, s)
        return jnp.max(top, axis=1, keepdims=True) * scale

    def weigh(t, u, slots, peak):
        base = pl.multiple_of(t * TILE, TILE)
        count = count_ref[t]
        if last:
            old = stat_ref[pl.ds(base, TILE), :]
            before = old[:, 0:1]
            peak = jnp.where(count > 0, jnp.maximum(peak, before), before)
        done = None
        for j in range(0, slots, 2):
            spots = [pl.multiple_of(index_ref[t, j + h] * TILE, TILE) for h in range(2)]
            e = jnp.exp2(score_ref[u, j // 2] * scale - peak).astype(BF)
            e = jnp.concatenate([jnp.where(j + h < count, e[:, h * TILE : (h + 1) * TILE], none) for h in range(2)], axis=1)
            v = jnp.concatenate([win_ref[pl.ds(s, TILE), TILE:] for s in spots], axis=0)
            part = jnp.dot(e, jnp.concatenate([v, ones], axis=1), preferred_element_type=F32)
            done = part if done is None else done + part
        value, total = done[:, :TILE], done[:, TILE:]
        if last:
            shrink = jnp.exp2(before - peak)
            total = total + shrink * old[:, 1:2]
            value = value + shrink * old_ref[pl.ds(base, TILE), :]
            out_ref[pl.ds(base, TILE), :] = (value / total).astype(BF)
        else:
            peak = jnp.where(count > 0, peak, -1e30)
            out_ref[pl.ds(base, TILE), :] = value
            lane = lax.broadcasted_iota(jnp.int32, (TILE, TILE), 1)
            stat_ref[pl.ds(base, TILE), :] = jnp.where(lane == 0, peak, total)

    def step(i, carry):
        tiles = [i * together + u for u in range(together)]
        most = functools.reduce(jnp.maximum, [count_ref[t] for t in tiles])
        for k, slots in enumerate(sizes):
            fits = most <= slots
            if k > 0:
                fits = jnp.logical_and(fits, most > sizes[k - 1])

            @pl.when(fits)
            def _(slots=slots):
                peaks = [look(t, u, slots) for u, t in enumerate(tiles)]
                for u, t in enumerate(tiles):
                    weigh(t, u, slots, peaks[u])

        return carry

    lax.fori_loop(0, q_ref.shape[0] // TILE // together, step, 0)


def attend(index, count, q, frames, sizes, old=None, together=2):
    n, slots = q.shape[0], index.shape[1]
    rows = sum(f.shape[0] for f in frames)
    wide = jax.ShapeDtypeStruct((n, TILE), F32)
    return pl.pallas_call(
        functools.partial(attend_kernel, sizes, together, len(frames), old is not None),
        out_shape=(wide, wide) if old is None else jax.ShapeDtypeStruct((n, TILE), BF),
        in_specs=[WHOLE_SM] * 2 + [WHOLE_VM] + [WHOLE_ANY] * len(frames) + [WHOLE_VM] * (0 if old is None else 2),
        out_specs=(WHOLE_VM,) * 2 if old is None else WHOLE_VM,
        scratch_shapes=[
            VM((rows, 2 * TILE), BF),
            VM((together, sizes[-1] // 2, TILE, 2 * TILE), F32),
            pltpu.SemaphoreType.DMA((len(frames),)),
        ],
        compiler_params=pltpu.CompilerParams(vmem_limit_bytes=24 << 20),
        cost_estimate=pl.CostEstimate(
            flops=4 * 4 * n * slots * TILE * TILE, bytes_accessed=6 << 20, transcendentals=n * slots * TILE
        ),
    )(index, count, q, *frames, *(old or ()))


def project_kernel(order_ref, att_ref, *refs):
    weights, (mine_ref, other_ref, w_ref, sems) = refs[:-4], refs[-4:]
    chips, width, groups = att_ref.shape[0], mine_ref.shape[1], 3
    span = width // groups
    pieces = len(weights)
    loads = []
    for g in range(groups):
        columns, start = slice(g * span, (g + 1) * span), 0
        for b, ref in enumerate(weights):
            target = w_ref.at[pl.ds(start, ref.shape[0]), columns]
            loads.append(pltpu.make_async_copy(ref.at[:, columns], target, sems.at[g * pieces + b]))
            start += ref.shape[0]
    for copy in loads:
        copy.start()
    own = pl.multiple_of(order_ref[chips] * TILE, TILE)
    away = pl.multiple_of(TILE - own, TILE)
    mine = jnp.concatenate([att_ref[order_ref[b], pl.ds(own, TILE), :] for b in range(chips)], axis=1)
    other = jnp.concatenate([att_ref[order_ref[b], pl.ds(away, TILE), :] for b in range(chips)], axis=1)
    left = jnp.concatenate([mine, other], axis=0)
    for g in range(groups):
        for copy in loads[g * pieces : (g + 1) * pieces]:
            copy.wait()
        for column in range(g * span, (g + 1) * span, 256):
            done = jnp.dot(left, w_ref[:, column : column + 256], preferred_element_type=F32)
            mine_ref[:, column : column + 256] = done[:TILE]
            other_ref[:, column : column + 256] = done[TILE:].astype(BF)


def project(order, attended, weights):
    width, rows = weights[0].shape[1], sum(w.shape[0] for w in weights)
    return pl.pallas_call(
        project_kernel,
        out_shape=(jax.ShapeDtypeStruct((TILE, width), F32), jax.ShapeDtypeStruct((TILE, width), BF)),
        in_specs=[WHOLE_SM, WHOLE_VM] + [WHOLE_HBM] * len(weights),
        out_specs=(WHOLE_VM,) * 2,
        scratch_shapes=[VM((rows, width), BF), pltpu.SemaphoreType.DMA((3 * len(weights),))],
        compiler_params=pltpu.CompilerParams(vmem_limit_bytes=24 << 20),
        cost_estimate=pl.CostEstimate(flops=4 * TILE * 8 * TILE * width, bytes_accessed=10 << 20, transcendentals=0),
    )(order, attended, *in_hbm(weights))


def listed(place, chosen, slots):
    before = jnp.arange(place.shape[1])[None, :] < jnp.arange(place.shape[1])[:, None]
    rank = jnp.sum(jnp.where(before[None] & chosen[:, None, :], 1, 0), axis=2)
    count = jnp.sum(chosen.astype(jnp.int32), axis=1)
    lead = jnp.minimum(jnp.arange(slots)[None, :], jnp.maximum(count - 1, 0)[:, None])
    lead = jnp.where(jnp.arange(slots)[None, :] < count[:, None], lead, 0)
    hit = (rank[:, None, :] == lead[:, :, None]) & chosen[:, None, :]
    return jnp.sum(jnp.where(hit, place[:, None, :], 0), axis=2).astype(jnp.int32), count


def body(tokens, w_qkv, w_out, source_row, key_tiles, key_count):
    z, yl = lax.axis_index("z"), lax.axis_index("yl")
    yh, x, core = lax.axis_index("yh"), lax.axis_index("x"), lax.axis_index("core")
    after = lax.optimization_barrier

    def chips(part):
        return [((yh + dy) % 2) * 4 + (x + 4 - dx) % 4 for dy, dx in part]

    def blocks(part):
        return jnp.stack([2 * c + side for side in (core, 1 - core) for c in chips(part)]).astype(F32)

    one, three = round_x(tokens, 1), round_x(tokens, -1)
    far_own = swap(tokens, "yh")
    w_other = swap(w_qkv, "core")
    half = tokens.shape[0] // 2
    low, high = round_x(one[:half], 1), round_x(three[half:], -1)
    far_next, _ = after((far_own, (one, three)))
    f_one, f_three = round_x(far_next, 1), round_x(far_next, -1)
    far_two = swap(jnp.concatenate([low, high], axis=0), "yh")
    near_mine, near_theirs = qkv(w_qkv, w_other, [tokens, one, three, far_own])
    near_other = swap(near_theirs, "core")
    want = source_row[0][:, None]
    near = place_near(blocks(NEAR), want, near_mine, near_other)
    tiles, slots = key_tiles.shape
    relative = key_tiles - ((z * 2 + yl) - 2) * tiles
    frame, inside = relative // tiles, relative % tiles
    crossing = frame == jnp.where(yl == 0, 1, 3)
    window = jnp.where(frame == 2, 0, jnp.where(frame == 0, 1, jnp.where(frame == 4, 3, 2)))
    valid = jnp.arange(slots)[None, :] < key_count[:, None]
    index, count = listed(window * tiles + inside, valid & ~crossing, slots)
    cross_index, cross_count = listed(inside, valid & crossing, tiles)
    lists = (index, count, cross_index, cross_count)
    far_two, near, (index, count, cross_index, cross_count) = after((far_two, near, lists))
    far_mine, far_theirs = qkv(w_qkv, w_other, [low, high, f_one, f_three, far_two])
    far_other = swap(far_theirs, "core")

    w_start, _ = after((w_out, near))
    w_one, w_three = round_x(w_start, 1), round_x(w_start, -1)
    w_far = opposite(w_start)
    w_turn, _ = after((w_out, far_two))
    w_two = round_x(w_turn, 2)

    q, kv = place_far(blocks(FAR), want, far_mine, far_other, near)
    kv, _ = after((kv, (w_one, w_three, w_far)))
    behind = lax.ppermute(kv, "z", [(i, (i + 1) % 8) for i in range(8)])
    ahead = lax.ppermute(kv, "z", [(i, (i + 7) % 8) for i in range(8)])
    beside = swap(kv, "yl")

    wf_pair = opposite(jnp.concatenate([w_one, w_three], axis=0))

    mid = kv.shape[0] // 2
    cross_low = swap(jnp.where(yl == 0, ahead[:mid], behind[:mid]), "yl")
    onward = [(2 * i, 2 * ((i + 1) % 8)) for i in range(8)] + [(2 * i + 1, 2 * ((i + 7) % 8) + 1) for i in range(8)]
    cross_high = lax.ppermute(beside[mid:], CTX, onward)

    state = attend(index, count, q, [kv, behind, beside, ahead], (24, slots), together=4)
    w_last, _ = after((w_far, state))
    wf_two = round_x(w_last, 2)
    attended = attend(cross_index, cross_count, q, [cross_low, cross_high], (6, tiles), state, together=4)

    pieces = lax.all_to_all(attended.reshape(8, 2 * TILE, TILE), CHIPS, split_axis=0, concat_axis=0, tiled=True)
    order = jnp.stack(chips(((0, 0), (0, 1), (0, 3), (0, 2), (1, 0), (1, 1), (1, 3), (1, 2))) + [core]).astype(jnp.int32)
    weights = [w_out, w_one, w_three, w_two, w_far, wf_pair, wf_two]
    mine, other = project(order, pieces, weights)
    return (mine + swap(other, "core").astype(F32)).astype(BF)


def solution(mesh):
    fine = Mesh(mesh.devices.reshape(8, 2, 2, 4, 2), ALL)
    in_specs = (
        P(ALL, None),
        P(None, ("yh", "x", "core")),
        P(("yh", "x", "core"), None),
        P(CTX, None),
        P(CTX, None),
        P(CTX),
    )
    return jax.shard_map(body, mesh=fine, in_specs=in_specs, out_specs=P(ALL, None), check_vma=False)
```

```python
import functools
import math

import jax
import jax.numpy as jnp
from jax import lax
from jax.experimental import pallas as pl
from jax.experimental.pallas import tpu as pltpu
from jax.sharding import Mesh
from jax.sharding import PartitionSpec as P

BF = jnp.bfloat16
F32 = jnp.float32
TILE = 128
LOG2E = 1.4426950408889634
VM = pltpu.VMEM
SM = pltpu.SMEM
CTX = ("z", "yl")
CHIPS = ("yh", "x")
ALL = ("z", "yl", "yh", "x", "core")
NEAR = ((0, 0), (0, 1), (0, 3), (1, 0))
FAR = ((0, 2), (1, 1), (1, 3), (1, 2))
WHOLE_VM = pl.BlockSpec(memory_space=VM)
WHOLE_SM = pl.BlockSpec(memory_space=SM)
WHOLE_ANY = pl.BlockSpec(memory_space=pl.ANY)
WHOLE_HBM = pl.BlockSpec(memory_space=pltpu.HBM)


def in_hbm(arrays):
    return [pltpu.with_memory_space_constraint(a, pltpu.HBM) for a in arrays]


def round_x(array, by):
    return lax.ppermute(array, "x", [(i, (i + by) % 4) for i in range(4)])


def swap(array, axis):
    return lax.ppermute(array, axis, [(0, 1), (1, 0)])


def opposite(array):
    return lax.ppermute(array, ("yl", "yh"), [(i, 3 - i) for i in range(4)])


def qkv_kernel(chunks, own_ref, other_ref, *refs):
    pieces, (mine_ref, theirs_ref, w_ref, sum_ref, sems) = refs[:-5], refs[-5:]
    width = mine_ref.shape[1]
    span = own_ref.shape[0] // chunks
    loads = []
    for c in range(chunks):
        depth = pl.ds(c * span, span)
        for side, ref in enumerate((other_ref, own_ref)):
            target = w_ref.at[depth, side * width : (side + 1) * width]
            loads.append(pltpu.make_async_copy(ref.at[depth, :], target, sems.at[2 * c + side]))
    for copy in loads:
        copy.start()
    for c in range(chunks):
        depth = slice(c * span, (c + 1) * span)
        rows = jnp.concatenate([piece[:, depth] for piece in pieces], axis=0)
        loads[2 * c].wait()
        loads[2 * c + 1].wait()
        done = jnp.dot(rows, w_ref[depth, :], preferred_element_type=F32)
        if c > 0:
            done = done + sum_ref[...]
        if c < chunks - 1:
            sum_ref[...] = done
    theirs_ref[...] = done[:, :width].astype(BF)
    mine_ref[...] = done[:, width:].astype(BF)


def qkv(own, other, pieces):
    n, depth, width, chunks = sum(p.shape[0] for p in pieces), own.shape[0], own.shape[1], 3
    return pl.pallas_call(
        functools.partial(qkv_kernel, chunks),
        out_shape=(jax.ShapeDtypeStruct((n, width), BF),) * 2,
        in_specs=[WHOLE_HBM] * 2 + [WHOLE_VM] * len(pieces),
        out_specs=(WHOLE_VM,) * 2,
        scratch_shapes=[
            VM((depth, 2 * width), BF),
            VM((n, 2 * width), F32),
            pltpu.SemaphoreType.DMA((2 * chunks,)),
        ],
        compiler_params=pltpu.CompilerParams(vmem_limit_bytes=24 << 20),
        cost_estimate=pl.CostEstimate(flops=4 * n * depth * width, bytes_accessed=8 << 20, transcendentals=0),
    )(*in_hbm((own, other)), *pieces)


def hot_rows(want, block_ref):
    n = want.shape[0]
    want = jnp.broadcast_to(want, (n, TILE))
    high = lax.shift_right_logical(want, 7).astype(F32).astype(BF)
    low = want & (TILE - 1)
    inside = jnp.where(low == lax.broadcasted_iota(jnp.int32, (n, TILE), 1), 1.0, 0.0).astype(BF)
    zero = jnp.zeros((n, TILE), BF)
    picks = [jnp.where(high == block_ref[b].astype(BF), inside, zero) for b in range(block_ref.shape[0])]
    return jnp.concatenate(picks, axis=1)


def pick(want, block_ref, first_ref, second_ref, columns=slice(None)):
    hot, half = hot_rows(want, block_ref), first_ref.shape[0]
    done = jnp.dot(hot[:, :half], first_ref[:, columns], preferred_element_type=F32)
    return done + jnp.dot(hot[:, half:], second_ref[:, columns], preferred_element_type=F32)


def place_near_kernel(block_ref, want_ref, first_ref, second_ref, out_ref):
    rows = 512

    def step(i, carry):
        spot = pl.ds(pl.multiple_of(i * rows, rows), rows)
        out_ref[spot, :] = pick(want_ref[spot, :], block_ref, first_ref, second_ref).astype(BF)
        return carry

    lax.fori_loop(0, want_ref.shape[0] // rows, step, 0)


def place_far_kernel(block_ref, want_ref, first_ref, second_ref, near_ref, q_ref, kv_ref, before_ref, sems):
    rows = 512
    steps = want_ref.shape[0] // rows
    copies = [
        pltpu.make_async_copy(near_ref.at[pl.ds(i * rows, rows)], before_ref.at[pl.ds(i * rows, rows)], sems.at[i])
        for i in range(steps)
    ]
    for copy in copies:
        copy.start()
    for i, copy in enumerate(copies):
        spot = slice(i * rows, (i + 1) * rows)
        done = pick(want_ref[spot, :], block_ref, first_ref, second_ref)
        copy.wait()
        done = done + before_ref[spot, :].astype(F32)
        q_ref[spot, :] = done[:, :TILE].astype(BF)
        kv_ref[spot, TILE:] = done[:, 2 * TILE :].astype(BF)
        for t in range(0, rows, TILE):
            keys = done[t : t + TILE, TILE : 2 * TILE]
            kv_ref[i * rows + t : i * rows + t + TILE, :TILE] = keys.T.astype(BF)


def place_near(blocks, want, first, second):
    n, width = want.shape[0], first.shape[1]
    return pl.pallas_call(
        place_near_kernel,
        out_shape=jax.ShapeDtypeStruct((n, width), BF),
        in_specs=[WHOLE_SM] + [WHOLE_VM] * 3,
        out_specs=WHOLE_VM,
        compiler_params=pltpu.CompilerParams(vmem_limit_bytes=24 << 20),
        cost_estimate=pl.CostEstimate(flops=n * n * width, bytes_accessed=4 << 20, transcendentals=0),
    )(blocks, want, first, second)


def place_far(blocks, want, first, second, near):
    n, width = want.shape[0], first.shape[1]
    return pl.pallas_call(
        place_far_kernel,
        out_shape=(pltpu.HBM((n, TILE), BF), jax.ShapeDtypeStruct((n, width - TILE), BF)),
        in_specs=[WHOLE_SM] + [WHOLE_VM] * 3 + [WHOLE_ANY],
        out_specs=(WHOLE_VM,) * 2,
        scratch_shapes=[VM((n, width), BF), pltpu.SemaphoreType.DMA((4,))],
        compiler_params=pltpu.CompilerParams(vmem_limit_bytes=24 << 20),
        cost_estimate=pl.CostEstimate(flops=n * n * width, bytes_accessed=4 << 20, transcendentals=0),
    )(blocks, want, first, second, *in_hbm((near,)))


def attend_kernel(sizes, together, parts, last, index_ref, count_ref, q_ref, *refs):
    frames = refs[:parts]
    refs = refs[parts:]
    if last:
        old_ref, stat_ref, out_ref = refs[:3]
    else:
        out_ref, stat_ref = refs[:2]
    win_ref, score_ref, sems = refs[-3:]
    copies, start = [], 0
    for i, frame in enumerate(frames):
        copies.append(pltpu.make_async_copy(frame, win_ref.at[pl.ds(start, frame.shape[0])], sems.at[i]))
        start += frame.shape[0]
    for copy in copies:
        copy.start()
    for copy in copies:
        copy.wait()
    scale = LOG2E / math.sqrt(TILE)

    ones = jnp.ones((2 * TILE, TILE), BF)
    none = jnp.zeros((TILE, TILE), BF)

    def look(t, u, slots):
        q = q_ref[pl.ds(pl.multiple_of(t * TILE, TILE), TILE), :]
        top = None
        for j in range(0, slots, 2):
            spots = [pl.multiple_of(index_ref[t, j + h] * TILE, TILE) for h in range(2)]
            k = jnp.concatenate([win_ref[pl.ds(s, TILE), :TILE] for s in spots], axis=1)
            s = jnp.dot(q, k, preferred_element_type=F32)
            score_ref[u, j // 2] = s
            s = jnp.maximum(s[:, :TILE], s[:, TILE:])
            top = s if top is None else jnp.maximum(top, s)
        return jnp.max(top, axis=1, keepdims=True) * scale

    def weigh(t, u, slots, peak):
        base = pl.multiple_of(t * TILE, TILE)
        count = count_ref[t]
        if last:
            old = stat_ref[pl.ds(base, TILE), :]
            before = old[:, 0:1]
            peak = jnp.where(count > 0, jnp.maximum(peak, before), before)
        done = None
        for j in range(0, slots, 2):
            spots = [pl.multiple_of(index_ref[t, j + h] * TILE, TILE) for h in range(2)]
            e = jnp.exp2(score_ref[u, j // 2] * scale - peak).astype(BF)
            e = jnp.concatenate([jnp.where(j + h < count, e[:, h * TILE : (h + 1) * TILE], none) for h in range(2)], axis=1)
            v = jnp.concatenate([win_ref[pl.ds(s, TILE), TILE:] for s in spots], axis=0)
            part = jnp.dot(e, jnp.concatenate([v, ones], axis=1), preferred_element_type=F32)
            done = part if done is None else done + part
        value, total = done[:, :TILE], done[:, TILE:]
        if last:
            shrink = jnp.exp2(before - peak)
            total = total + shrink * old[:, 1:2]
            value = value + shrink * old_ref[pl.ds(base, TILE), :]
            out_ref[pl.ds(base, TILE), :] = (value / total).astype(BF)
        else:
            peak = jnp.where(count > 0, peak, -1e30)
            out_ref[pl.ds(base, TILE), :] = value
            lane = lax.broadcasted_iota(jnp.int32, (TILE, TILE), 1)
            stat_ref[pl.ds(base, TILE), :] = jnp.where(lane == 0, peak, total)

    def step(i, carry):
        tiles = [i * together + u for u in range(together)]
        most = functools.reduce(jnp.maximum, [count_ref[t] for t in tiles])
        for k, slots in enumerate(sizes):
            fits = most <= slots
            if k > 0:
                fits = jnp.logical_and(fits, most > sizes[k - 1])

            @pl.when(fits)
            def _(slots=slots):
                peaks = [look(t, u, slots) for u, t in enumerate(tiles)]
                for u, t in enumerate(tiles):
                    weigh(t, u, slots, peaks[u])

        return carry

    lax.fori_loop(0, q_ref.shape[0] // TILE // together, step, 0)


def attend(index, count, q, frames, sizes, old=None, together=2):
    n, slots = q.shape[0], index.shape[1]
    rows = sum(f.shape[0] for f in frames)
    wide = jax.ShapeDtypeStruct((n, TILE), F32)
    return pl.pallas_call(
        functools.partial(attend_kernel, sizes, together, len(frames), old is not None),
        out_shape=(wide, wide) if old is None else jax.ShapeDtypeStruct((n, TILE), BF),
        in_specs=[WHOLE_SM] * 2 + [WHOLE_VM] + [WHOLE_ANY] * len(frames) + [WHOLE_VM] * (0 if old is None else 2),
        out_specs=(WHOLE_VM,) * 2 if old is None else WHOLE_VM,
        scratch_shapes=[
            VM((rows, 2 * TILE), BF),
            VM((together, sizes[-1] // 2, TILE, 2 * TILE), F32),
            pltpu.SemaphoreType.DMA((len(frames),)),
        ],
        compiler_params=pltpu.CompilerParams(vmem_limit_bytes=24 << 20),
        cost_estimate=pl.CostEstimate(
            flops=4 * 4 * n * slots * TILE * TILE, bytes_accessed=6 << 20, transcendentals=n * slots * TILE
        ),
    )(index, count, q, *frames, *(old or ()))


def project_kernel(early, order_ref, att_ref, *refs):
    weights, (mine_ref, other_ref, w_ref, sems) = refs[:-4], refs[-4:]
    chips, width, groups = att_ref.shape[0], mine_ref.shape[1], 3
    span = width // groups
    loads = []
    for g in range(groups):
        columns = slice(g * span, (g + 1) * span)
        for i, b in enumerate(early):
            loads.append(pltpu.make_async_copy(weights[b].at[:, columns], w_ref.at[i, :, columns], sems.at[g * len(early) + i]))
    for copy in loads:
        copy.start()
    own = pl.multiple_of(order_ref[chips] * TILE, TILE)
    away = pl.multiple_of(TILE - own, TILE)
    mine = jnp.concatenate([att_ref[order_ref[b], pl.ds(own, TILE), :] for b in range(chips)], axis=1)
    other = jnp.concatenate([att_ref[order_ref[b], pl.ds(away, TILE), :] for b in range(chips)], axis=1)
    left = jnp.concatenate([mine, other], axis=0)
    step = 256
    for g in range(groups):
        for copy in loads[g * len(early) : (g + 1) * len(early)]:
            copy.wait()
        for column in range(g * span, (g + 1) * span, step):
            columns = slice(column, column + step)
            right = [w_ref[early.index(b), :, columns] if b in early else w[:, columns] for b, w in enumerate(weights)]
            done = jnp.dot(left, jnp.concatenate(right, axis=0), preferred_element_type=F32)
            mine_ref[:, columns] = done[:TILE]
            other_ref[:, columns] = done[TILE:].astype(BF)


def project(order, attended, weights, early):
    width = weights[0].shape[1]
    spaces = [pltpu.HBM if b in early else pltpu.VMEM for b in range(len(weights))]
    weights = [pltpu.with_memory_space_constraint(w, space) for w, space in zip(weights, spaces)]
    return pl.pallas_call(
        functools.partial(project_kernel, early),
        out_shape=(jax.ShapeDtypeStruct((TILE, width), F32), jax.ShapeDtypeStruct((TILE, width), BF)),
        in_specs=[WHOLE_SM, WHOLE_VM] + [WHOLE_HBM if b in early else WHOLE_VM for b in range(len(weights))],
        out_specs=(WHOLE_VM,) * 2,
        scratch_shapes=[VM((len(early), TILE, width), BF), pltpu.SemaphoreType.DMA((3 * len(early),))],
        compiler_params=pltpu.CompilerParams(vmem_limit_bytes=24 << 20),
        cost_estimate=pl.CostEstimate(flops=4 * TILE * 8 * TILE * width, bytes_accessed=10 << 20, transcendentals=0),
    )(order, attended, *weights)


def listed(place, chosen, slots):
    before = jnp.arange(place.shape[1])[None, :] < jnp.arange(place.shape[1])[:, None]
    rank = jnp.sum(jnp.where(before[None] & chosen[:, None, :], 1, 0), axis=2)
    count = jnp.sum(chosen.astype(jnp.int32), axis=1)
    lead = jnp.minimum(jnp.arange(slots)[None, :], jnp.maximum(count - 1, 0)[:, None])
    lead = jnp.where(jnp.arange(slots)[None, :] < count[:, None], lead, 0)
    hit = (rank[:, None, :] == lead[:, :, None]) & chosen[:, None, :]
    return jnp.sum(jnp.where(hit, place[:, None, :], 0), axis=2).astype(jnp.int32), count


def body(tokens, w_qkv, w_out, source_row, key_tiles, key_count):
    z, yl = lax.axis_index("z"), lax.axis_index("yl")
    yh, x, core = lax.axis_index("yh"), lax.axis_index("x"), lax.axis_index("core")
    after = lax.optimization_barrier

    def chips(part):
        return [((yh + dy) % 2) * 4 + (x + 4 - dx) % 4 for dy, dx in part]

    def blocks(part):
        return jnp.stack([2 * c + side for side in (core, 1 - core) for c in chips(part)]).astype(F32)

    one, three = round_x(tokens, 1), round_x(tokens, -1)
    far_own = swap(tokens, "yh")
    w_other = swap(w_qkv, "core")
    half = tokens.shape[0] // 2
    low, high = round_x(one[:half], 1), round_x(three[half:], -1)
    far_next, _ = after((far_own, (one, three)))
    f_one, f_three = round_x(far_next, 1), round_x(far_next, -1)
    far_two = swap(jnp.concatenate([low, high], axis=0), "yh")
    near_mine, near_theirs = qkv(w_qkv, w_other, [tokens, one, three, far_own])
    near_other = swap(near_theirs, "core")
    want = source_row[0][:, None]
    near = place_near(blocks(NEAR), want, near_mine, near_other)
    tiles, slots = key_tiles.shape
    relative = key_tiles - ((z * 2 + yl) - 2) * tiles
    frame, inside = relative // tiles, relative % tiles
    crossing = frame == jnp.where(yl == 0, 1, 3)
    window = jnp.where(frame == 2, 0, jnp.where(frame == 0, 1, jnp.where(frame == 4, 3, 2)))
    valid = jnp.arange(slots)[None, :] < key_count[:, None]
    index, count = listed(window * tiles + inside, valid & ~crossing, slots)
    cross_index, cross_count = listed(inside, valid & crossing, tiles)
    lists = (index, count, cross_index, cross_count)
    far_two, near, (index, count, cross_index, cross_count) = after((far_two, near, lists))
    far_mine, far_theirs = qkv(w_qkv, w_other, [low, high, f_one, f_three, far_two])
    far_other = swap(far_theirs, "core")

    w_start, _ = after((w_out, near))
    w_one, w_three = round_x(w_start, 1), round_x(w_start, -1)
    w_far = opposite(w_start)
    w_turn, _ = after((w_out, far_two))
    w_two = round_x(w_turn, 2)

    q, kv = place_far(blocks(FAR), want, far_mine, far_other, near)
    kv, _ = after((kv, (w_one, w_three, w_far)))
    behind = lax.ppermute(kv, "z", [(i, (i + 1) % 8) for i in range(8)])
    ahead = lax.ppermute(kv, "z", [(i, (i + 7) % 8) for i in range(8)])
    beside = swap(kv, "yl")

    wf_pair = opposite(jnp.concatenate([w_one, w_three], axis=0))

    mid = kv.shape[0] // 2
    cross_low = swap(jnp.where(yl == 0, ahead[:mid], behind[:mid]), "yl")
    onward = [(2 * i, 2 * ((i + 1) % 8)) for i in range(8)] + [(2 * i + 1, 2 * ((i + 7) % 8) + 1) for i in range(8)]
    cross_high = lax.ppermute(beside[mid:], CTX, onward)

    state = attend(index, count, q, [kv, behind, beside, ahead], (24, slots), together=4)
    w_last, _ = after((w_far, state))
    wf_two = round_x(w_last, 2)
    attended = attend(cross_index, cross_count, q, [cross_low, cross_high], (6, tiles), state, together=4)

    pieces = lax.all_to_all(attended.reshape(8, 2 * TILE, TILE), CHIPS, split_axis=0, concat_axis=0, tiled=True)
    order = jnp.stack(chips(((0, 0), (0, 1), (0, 3), (0, 2), (1, 0), (1, 1), (1, 3), (1, 2))) + [core]).astype(jnp.int32)
    weights = [w_out, w_one, w_three, w_two, w_far, wf_pair, wf_two]
    mine, other = project(order, pieces, weights, (0, 1, 2, 4))
    return (mine + swap(other, "core").astype(F32)).astype(BF)


def solution(mesh):
    fine = Mesh(mesh.devices.reshape(8, 2, 2, 4, 2), ALL)
    in_specs = (
        P(ALL, None),
        P(None, ("yh", "x", "core")),
        P(("yh", "x", "core"), None),
        P(CTX, None),
        P(CTX, None),
        P(CTX),
    )
    return jax.shard_map(body, mesh=fine, in_specs=in_specs, out_specs=P(ALL, None), check_vma=False)
```
